256 devices in a mesh: blk: 32 (over y_lo, z, core), inner: 8 (over y_hi, x).
Axes of the slice: x: 4, y: 4 (y_hi: 2, y_lo: 2; y = y_hi * 2 + y_lo), z: 8, core: 2. Of those that a mesh axis runs over, the one named last changes fastest.
Arguments:
- queries: bfloat16 [6144, 5120], P('blk', 'inner'), may hold values from -48 to 48
- keys: bfloat16 [6144, 1024], P('blk', 'inner'), may hold values from -48 to 48
- values: bfloat16 [6144, 1024], P('blk', 'inner'), may hold values from -6 to 6
- positions: int32 [6144], P('blk'), may hold values from 0 to 6143, as said below
- out_weight: bfloat16 [5120, 5120], P('inner'), may hold values from -0.078125 to 0.078125
Outputs:
- projected: bfloat16 [6144, 5120], P(('blk', 'inner'))
The draws below stay inside these ranges and needn't reach their ends.
Inputs may be any that keep to these rules, and one draw needn't show every extreme that they name: The rows of index b of blk (rows 192 b to 192 b + 191) hold the positions c * 96 to c * 96 + 95 followed by (63 - c) * 96 to (63 - c) * 96 + 95, in increasing order, with a different c from 0 to 31 for every b; every position appears once.
All inputs are finite; a program needn't handle non-finite values.
Results may differ from the reference program's by a relative error of at most 0.018.
Values may be sent and summed in bfloat16 or wider, within the bound.
A program may use at most 128 MiB of HBM per device.

```python
import math
import jax
import jax.numpy as jnp
from jax import lax

D = 5120
HEAD_WIDTH = 128
KEY_VALUE_HEADS = 8
QUERY_PER_KEY = 5
HQ = 40
CH = 96
TOKEN_LENGTH = 6144
N_INNER = 8


def starting_field(key, shape):
    return jnp.clip(jax.random.normal(key, shape, jnp.float32), -6.0, 6.0)


def draw_queries(key, part):
    field_vector = starting_field(jax.random.fold_in(key, 1), (TOKEN_LENGTH, KEY_VALUE_HEADS, QUERY_PER_KEY, HEAD_WIDTH))
    return field_vector.reshape(TOKEN_LENGTH, KEY_VALUE_HEADS * QUERY_PER_KEY * HEAD_WIDTH).astype(jnp.bfloat16)


def draw_keys(key, part):
    field_vector = starting_field(jax.random.fold_in(key, 2), (TOKEN_LENGTH, KEY_VALUE_HEADS, HEAD_WIDTH))
    return field_vector.reshape(TOKEN_LENGTH, KEY_VALUE_HEADS * HEAD_WIDTH).astype(jnp.bfloat16)


def draw_positions(key, part):
    pair_count = TOKEN_LENGTH // (2 * CH)
    order = jax.random.permutation(key, pair_count)
    slot_ids = jnp.arange(2 * CH)
    early = order[:, None] * CH + slot_ids[None, :]
    late = (2 * pair_count - 1 - order[:, None]) * CH + slot_ids[None, :] - CH
    return jnp.where(slot_ids[None, :] < CH, early, late).reshape(TOKEN_LENGTH).astype(jnp.int32)


def shard_levels(key, shape, cuts, low, largest):
    gain, own = 1.0, jax.random.fold_in(key, 6)
    for dim, parts in cuts:
        heights = jnp.exp(jax.random.uniform(jax.random.fold_in(own, dim), (parts,), jnp.float32, low / len(cuts), largest / len(cuts)))
        gain = gain * jnp.repeat(heights, shape[dim] // parts).reshape([-1 if axis == dim else 1 for axis in range(len(shape))])
    return gain


def scatter_about(rng, dims, deviation, most, split=(), kind=jnp.bfloat16):
    result = deviation * jax.random.normal(rng, dims, jnp.float32)
    if split:
        result = result * shard_levels(rng, dims, split, -0.22, 0.18)
    return jnp.clip(result, -most, most).astype(kind)


def setup_inputs(seed: int = 0) -> dict:
    arg_keys = jax.random.split(jax.random.key(seed), 6)
    return {
        "queries": draw_queries(jax.random.fold_in(arg_keys[5], 71), 0),
        "keys": draw_keys(jax.random.fold_in(arg_keys[5], 71), 0),
        "values": scatter_about(arg_keys[2], (TOKEN_LENGTH, KEY_VALUE_HEADS * HEAD_WIDTH), 1.0, 6.0, ((0, 32), (1, 8))),
        "positions": draw_positions(jax.random.fold_in(arg_keys[5], 71), 0),
        "out_weight": scatter_about(arg_keys[4], (HQ * HEAD_WIDTH, D), (HQ * HEAD_WIDTH) ** -0.5, 0.078125, ((0, 8),)),
    }


def reference(queries, keys, values, positions, out_weight):
    row_total = queries.shape[0]
    per_head_queries = jnp.transpose(queries.reshape(row_total, KEY_VALUE_HEADS * QUERY_PER_KEY, HEAD_WIDTH), (1, 0, 2))
    per_head_keys = jnp.repeat(jnp.transpose(keys.reshape(row_total, KEY_VALUE_HEADS, HEAD_WIDTH), (1, 0, 2)), QUERY_PER_KEY, axis=0)
    per_head_values = jnp.repeat(jnp.transpose(values.reshape(row_total, KEY_VALUE_HEADS, HEAD_WIDTH), (1, 0, 2)), QUERY_PER_KEY, axis=0)
    visible = positions[None, :] <= positions[:, None]
    inverse_root = 1.0 / math.sqrt(HEAD_WIDTH)

    def one_head(operands):
        query_head, key_head, value_head = operands
        scores = jnp.dot(query_head, key_head.T, preferred_element_type=jnp.float32) * inverse_root
        scores = jnp.where(visible, scores, -1e+30)
        highest = lax.optimization_barrier(jnp.max(scores, axis=1, keepdims=True))
        weights = jnp.where(visible, jnp.exp(scores - highest), 0.0)
        totals = lax.optimization_barrier(jnp.sum(weights, axis=1, keepdims=True))
        mixed = jnp.dot(weights.astype(jnp.bfloat16), value_head, preferred_element_type=jnp.float32)
        return (mixed / totals).astype(jnp.bfloat16)
    head_outputs = lax.map(one_head, (per_head_queries, per_head_keys, per_head_values))
    attended_values = jnp.transpose(head_outputs, (1, 0, 2)).reshape(row_total, KEY_VALUE_HEADS * QUERY_PER_KEY * HEAD_WIDTH)
    group_columns = KEY_VALUE_HEADS * QUERY_PER_KEY * HEAD_WIDTH // N_INNER
    summed = jnp.zeros((row_total, out_weight.shape[1]), jnp.float32)
    for group_id in range(N_INNER):
        part_cols = attended_values[:, group_id * group_columns:(group_id + 1) * group_columns]
        part_rows = out_weight[group_id * group_columns:(group_id + 1) * group_columns]
        partial_term = jnp.dot(part_cols, part_rows, preferred_element_type=jnp.float32).astype(jnp.bfloat16)
        summed = summed + partial_term.astype(jnp.float32)
    return summed.astype(jnp.bfloat16)
```

```python
import math

import jax
import jax.numpy as jnp
from jax import lax
from jax.experimental import pallas as pl
from jax.experimental.pallas import tpu as pltpu
from jax.sharding import PartitionSpec as P

MESH = pl.DeviceIdType.MESH
HEAD = 128
PER_KEY = 5
CH = 96
LANES = 512
SCALE = math.log2(math.e) / math.sqrt(HEAD)
LOW = -1e30

CHIPS = [
    (0, 0), (0, 1), (0, -1), (1, 0),
    (0, 2), (0, -2), (1, 1), (1, -1),
    (0, 3), (0, -3), (1, 2), (1, -2),
    (0, 4), (1, 3), (1, -3), (1, 4),
]
SLOT = {chip: 2 * j for j, chip in enumerate(CHIPS)}
GROUP = 8
ROWS = (208, 192)
SPLIT = (112, 96)
OWN = 24
HALF = 2560


def kernel(
    q_hbm, k_hbm, v_hbm, pos_ref, w_hbm, out_ref,
    q_in, w_in, early, late, q_t, high, total, acc, tri, part, gathered,
    load_sem, send_sem, recv_sem, half_sem, out_send, out_recv,
):
    blk, inner = lax.axis_index("blk"), lax.axis_index("inner")
    ylo, z, core = blk // 16, (blk // 2) % 8, blk % 2
    yhi, x = inner // 4, inner % 4
    bufs = (early, late)

    loads = [
        pltpu.make_async_copy(k_hbm.at[pl.ds(0, CH)], early.at[0, pl.ds(0, CH)], load_sem.at[0]),
        pltpu.make_async_copy(v_hbm.at[pl.ds(0, CH)], early.at[0, pl.ds(CH, CH)], load_sem.at[1]),
        pltpu.make_async_copy(k_hbm.at[pl.ds(CH, CH)], late.at[0, pl.ds(0, CH)], load_sem.at[2]),
        pltpu.make_async_copy(v_hbm.at[pl.ds(CH, CH)], late.at[0, pl.ds(CH, CH)], load_sem.at[3]),
        pltpu.make_async_copy(q_hbm, q_in, load_sem.at[4]),
        pltpu.make_async_copy(w_hbm, w_in, load_sem.at[5]),
    ]
    for load in loads:
        load.start()
    tag = pos_ref[0].astype(jnp.float32)
    early[0, pl.ds(2 * CH, 16), :] = jnp.full((16, HEAD), tag, jnp.float32).astype(jnp.bfloat16)

    def at(dy, dz, dc=0):
        y = ylo + dy - 2 * dy * ylo
        c = core + dc - 2 * dc * core
        return (y * 16 + lax.rem(z + dz + 8, 8) * 2 + c, inner)

    barrier = pltpu.get_barrier_semaphore()
    greeted = [at(0, 1), at(0, -1), at(0, 2), at(0, -2), at(1, 0), at(0, 0, 1)]
    greeted += [(blk, lax.rem(inner + d, 8)) for d in range(1, 8)]
    for device in greeted:
        pl.semaphore_signal(barrier, inc=1, device_id=device, device_id_type=MESH)

    sends = []

    def send(phase, src, dst, device, rows=None, half=False):
        count = sum(1 for p, _ in sends if p == phase)
        lo, size = rows or (0, ROWS[phase])
        buf = bufs[phase]
        copy = pltpu.make_async_remote_copy(
            src_ref=buf.at[src, pl.ds(lo, size)],
            dst_ref=buf.at[dst, pl.ds(lo, size)],
            send_sem=send_sem.at[phase, count],
            recv_sem=half_sem.at[phase] if half else recv_sem.at[phase, dst],
            device_id=device,
            device_id_type=MESH,
        )
        copy.start()
        sends.append((phase, copy))

    def arrived(phase, slot, rows=None, half=False):
        lo, size = rows or (0, ROWS[phase])
        ref = bufs[phase].at[slot, pl.ds(lo, size)]
        sem = half_sem.at[phase] if half else recv_sem.at[phase, slot]
        pltpu.make_async_copy(ref, ref, sem).wait()

    def halves(phase):
        return (0, SPLIT[phase]), (SPLIT[phase], ROWS[phase] - SPLIT[phase])

    def sibling(phase, chip):
        send(phase, SLOT[chip], SLOT[chip] + 1, at(0, 0, 1))

    def partner(phase, dz):
        send(phase, SLOT[0, dz], SLOT[1, dz], at(1, 0))

    def stage_one(phase):
        for d in (2, -2, 1, -1):
            send(phase, 0, SLOT[0, -d], at(0, d))
        partner(phase, 0)
        sibling(phase, (0, 0))

    def stage_two(phase):
        for d in (1, -1):
            arrived(phase, SLOT[0, d])
            partner(phase, d)
            sibling(phase, (0, d))
        first, second = halves(phase)
        for d in (2, -2):
            s = d // 2
            arrived(phase, SLOT[0, d])
            send(phase, SLOT[0, d], SLOT[0, 3 * s], at(0, -s))
            send(phase, SLOT[0, d], SLOT[0, 4], at(0, -d), first if s > 0 else second, half=s < 0)
            partner(phase, d)
            sibling(phase, (0, d))
        arrived(phase, SLOT[1, 0])
        sibling(phase, (1, 0))

    def stage_three(phase):
        for d in (1, -1, 2, -2):
            arrived(phase, SLOT[1, d])
            sibling(phase, (1, d))
        for d in (3, -3):
            arrived(phase, SLOT[0, d])
            partner(phase, d)
            sibling(phase, (0, d))
        first, second = halves(phase)
        arrived(phase, SLOT[0, 4], first)
        arrived(phase, SLOT[0, 4], second, half=True)
        partner(phase, 4)
        sibling(phase, (0, 4))

    def stage_four(phase):
        for d in (3, -3, 4):
            arrived(phase, SLOT[1, d])
            sibling(phase, (1, d))

    def from_sibling(phase, group):
        for j in range(4 * group, 4 * group + 4):
            arrived(phase, 2 * j + 1)

    def attend(phase, which, group, first=False):
        buf = bufs[which]
        base = group * GROUP
        keys = buf[pl.ds(base, GROUP), pl.ds(0, CH), :].reshape(GROUP * CH, HEAD)
        values = buf[pl.ds(base, GROUP), pl.ds(CH, CH), :].reshape(GROUP * CH, HEAD)
        scores = jnp.dot(keys, q_t[phase], preferred_element_type=jnp.float32)
        if phase == which:
            tags = early[pl.ds(base, GROUP), pl.ds(2 * CH, 16), :].astype(jnp.float32)[:, :1, :]
            seen = tags < tag if phase == 0 else tags > tag
            bias = jnp.where(seen, 0.0, LOW)
            bias = jnp.concatenate([bias] * (LANES // HEAD), axis=2)
            scores = scores.reshape(GROUP, CH, LANES)
            if first:
                scores = jnp.concatenate([scores[:1] + tri[...][None], scores[1:] + bias[1:]], axis=0)
            else:
                scores = scores + bias
            scores = scores.reshape(GROUP * CH, LANES)
        old = high[phase]
        new = jnp.maximum(old, jnp.max(scores, axis=0, keepdims=True) * SCALE)
        weights = jnp.exp2(scores * SCALE - new)
        keep = jnp.exp2(old - new)
        high[phase] = new
        total[phase] = total[phase] * keep + jnp.sum(weights, axis=0, keepdims=True)
        mixed = lax.dot_general(
            values, weights.astype(jnp.bfloat16), (((0,), (0,)), ((), ())),
            preferred_element_type=jnp.float32,
        )
        acc[phase] = acc[phase] * keep + mixed

    def attend_many(phase, which, lo, hi):
        def body(group, carry):
            attend(phase, which, group)
            return carry

        lax.fori_loop(lo, hi, body, 0)

    def project(phase):
        rows = jnp.transpose(acc[phase] * (1.0 / total[phase])).astype(jnp.bfloat16)
        rows = jnp.concatenate([rows[h * CH : (h + 1) * CH] for h in range(PER_KEY)], axis=1)

        def body(j, carry):
            lo = pl.multiple_of(j * 512, 512)
            left, right = [
                jnp.dot(
                    rows, w_in[:, pl.ds(pl.multiple_of(side * HALF + lo, 512), 512)],
                    preferred_element_type=jnp.float32,
                )
                for side in range(2)
            ]
            for d in range(4):
                cut = slice(OWN * d, OWN * (d + 1))
                both = jnp.concatenate([left[cut], right[cut]], axis=0)
                part[phase, d, :, pl.ds(lo, 512)] = both.astype(jnp.bfloat16)
            return carry

        lax.fori_loop(0, HALF // 512, body, 0)

    def share(phase, d):
        to = lax.rem(x + d, 4)
        other = yhi if phase == 0 else 1 - yhi
        return other, pltpu.make_async_remote_copy(
            src_ref=part.at[phase, to],
            dst_ref=gathered.at[other * 4 + (4 - d) % 4],
            send_sem=out_send.at[phase, d],
            recv_sem=out_recv.at[other * 4 + (4 - d) % 4],
            device_id=(blk, phase * 4 + to),
            device_id_type=MESH,
        )

    def scatter(phase, wait=False):
        for d in (2, 1, 3, 0):
            other, copy = share(phase, d)
            act = copy.wait_send if wait else copy.start
            if d:
                act()
            else:
                pl.when(other == 1)(act)

    lane = lax.broadcasted_iota(jnp.int32, (CH, LANES), 1)
    start = sum(jnp.where(lane >= CH * h, CH, 0) for h in range(1, PER_KEY + 1))
    row = lax.broadcasted_iota(jnp.int32, (CH, LANES), 0)
    tri[...] = jnp.where(row <= lane - start, 0.0, LOW)
    high[...] = jnp.full(high.shape, LOW, jnp.float32)
    total[...] = jnp.zeros(total.shape, jnp.float32)
    acc[...] = jnp.zeros(acc.shape, jnp.float32)

    pl.semaphore_wait(barrier, len(greeted))
    loads[0].wait()
    loads[1].wait()
    stage_one(0)
    loads[2].wait()
    loads[3].wait()
    stage_one(1)
    loads[4].wait()
    for phase in range(2):
        heads = [q_in[pl.ds(CH * phase, CH), pl.ds(HEAD * h, HEAD)] for h in range(PER_KEY)]
        pad = jnp.zeros((LANES - PER_KEY * CH, HEAD), jnp.bfloat16)
        q_t[phase] = jnp.transpose(jnp.concatenate(heads + [pad], axis=0))

    stage_two(0)
    stage_two(1)
    from_sibling(0, 0)
    attend(0, 0, 0, first=True)
    stage_three(0)
    from_sibling(0, 1)
    attend(0, 0, 1)
    stage_three(1)
    from_sibling(0, 2)
    attend(0, 0, 2)
    stage_four(0)
    from_sibling(0, 3)
    attend(0, 0, 3)
    loads[5].wait()
    project(0)
    scatter(0)
    stage_four(1)
    attend_many(1, 0, 0, 4)
    from_sibling(1, 0)
    attend(1, 1, 0, first=True)
    for group in range(1, 4):
        from_sibling(1, group)
    attend_many(1, 1, 1, 4)
    project(1)
    scatter(1)

    for _, copy in sends:
        copy.wait_send()
    scatter(0, wait=True)
    for s in range(1, 8):
        pltpu.make_async_copy(gathered.at[s], gathered.at[s], out_recv.at[s]).wait()

    def add_up(j, carry):
        cols = pl.ds(pl.multiple_of(j * 256, 256), 256)
        summed = part[yhi, x, :, cols].astype(jnp.float32)
        for s in range(1, 8):
            summed = summed + gathered[s, :, cols].astype(jnp.float32)
        summed = summed.astype(out_ref.dtype)
        out_ref[:, cols] = summed[:OWN]
        out_ref[:, pl.ds(pl.multiple_of(HALF + j * 256, 256), 256)] = summed[OWN:]
        return carry

    lax.fori_loop(0, HALF // 256, add_up, 0)
    scatter(1, wait=True)


def shards(queries, keys, values, positions, out_weight):
    any_space = pl.BlockSpec(memory_space=pl.ANY)
    return pl.pallas_call(
        kernel,
        out_shape=jax.ShapeDtypeStruct((OWN, 2 * HALF), jnp.bfloat16),
        in_specs=[any_space] * 3 + [pl.BlockSpec(memory_space=pltpu.SMEM), any_space],
        out_specs=pl.BlockSpec(memory_space=pltpu.VMEM),
        scratch_shapes=[
            pltpu.VMEM((2 * CH, PER_KEY * HEAD), jnp.bfloat16),
            pltpu.VMEM((PER_KEY * HEAD, 2 * HALF), jnp.bfloat16),
            pltpu.VMEM((32, ROWS[0], HEAD), jnp.bfloat16),
            pltpu.VMEM((32, ROWS[1], HEAD), jnp.bfloat16),
            pltpu.VMEM((2, HEAD, LANES), jnp.bfloat16),
            pltpu.VMEM((2, 1, LANES), jnp.float32),
            pltpu.VMEM((2, 1, LANES), jnp.float32),
            pltpu.VMEM((2, HEAD, LANES), jnp.float32),
            pltpu.VMEM((CH, LANES), jnp.float32),
            pltpu.VMEM((2, 4, 2 * OWN, HALF), jnp.bfloat16),
            pltpu.VMEM((8, 2 * OWN, HALF), jnp.bfloat16),
            pltpu.SemaphoreType.DMA((6,)),
            pltpu.SemaphoreType.DMA((2, 32)),
            pltpu.SemaphoreType.DMA((2, 32)),
            pltpu.SemaphoreType.DMA((2,)),
            pltpu.SemaphoreType.DMA((2, 4)),
            pltpu.SemaphoreType.DMA((8,)),
        ],
        compiler_params=pltpu.CompilerParams(
            collective_id=0, has_side_effects=True, vmem_limit_bytes=48 << 20
        ),
        cost_estimate=pl.CostEstimate(
            flops=4_000_000_000, bytes_accessed=10_000_000, transcendentals=5_000_000
        ),
    )(queries, keys, values, positions, out_weight)


def solution(mesh):
    placed = (P("blk", "inner"), P("blk", "inner"), P("blk", "inner"), P("blk"), P("inner", None))
    return jax.shard_map(
        shards, mesh=mesh, in_specs=placed, out_specs=P(("blk", "inner"), None), check_vma=False
    )
```

```python
import math

import jax
import jax.numpy as jnp
from jax import lax
from jax.experimental import pallas as pl
from jax.experimental.pallas import tpu as pltpu
from jax.sharding import PartitionSpec as P

MESH = pl.DeviceIdType.MESH
HEAD = 128
PER_KEY = 5
CH = 96
LANES = 512
SCALE = math.log2(math.e) / math.sqrt(HEAD)
LOW = -1e30

CHIPS = [
    (0, 0), (0, 1), (0, -1), (1, 0),
    (0, 2), (0, -2), (1, 1), (1, -1),
    (0, 3), (0, -3), (1, 2), (1, -2),
    (0, 4), (1, 3), (1, -3), (1, 4),
]
SLOT = {chip: 2 * j for j, chip in enumerate(CHIPS)}
GROUP = 8
ROWS = (208, 192)
OWN = 24
HALF = 2560
CHUNKS = 4
WIDE = HALF // CHUNKS


TREES = (
    {
        (0, 0): [(0, 2), (0, -2), (0, 1), (0, -1), (1, 0)],
        (0, 1): [(1, 1)],
        (0, -1): [(1, -1)],
        (0, 2): [(0, 3), (0, 4), (1, 2)],
        (0, -2): [(0, -3), (1, -2)],
        (1, 2): [(1, 3)],
        (1, -2): [(1, -3), (1, 4)],
    },
    {
        (0, 0): [(0, 1), (0, -1), (1, 0)],
        (0, 1): [(0, 2), (1, 1)],
        (0, -1): [(0, -2), (1, -1)],
        (0, 2): [(0, 3), (1, 2)],
        (0, -2): [(0, -3), (1, -2)],
        (0, 3): [(0, 4)],
        (1, 2): [(1, 3)],
        (1, -2): [(1, -3)],
        (1, -3): [(1, 4)],
    },
)


def slot_of(chip):
    dy, dz = chip
    return SLOT[dy, dz if dz == 4 else -dz]


def kernel(
    q_hbm, k_hbm, v_hbm, pos_hbm, w_hbm, out_ref,
    q_in, w_in, pos_in, early, late, q_t, high, total, acc, tri,
    part, through, passed, beside, across, crossed,
    load_sem, send_sem, recv_sem, row_send, row_recv,
):
    blk, inner = lax.axis_index("blk"), lax.axis_index("inner")
    ylo, z, core = blk // 16, (blk // 2) % 8, blk % 2
    yhi, x = inner // 4, inner % 4
    bufs = (early, late)

    loads = [
        pltpu.make_async_copy(pos_hbm, pos_in, load_sem.at[6]),
        pltpu.make_async_copy(k_hbm.at[pl.ds(0, CH)], early.at[0, pl.ds(0, CH)], load_sem.at[0]),
        pltpu.make_async_copy(v_hbm.at[pl.ds(0, CH)], early.at[0, pl.ds(CH, CH)], load_sem.at[1]),
        pltpu.make_async_copy(k_hbm.at[pl.ds(CH, CH)], late.at[0, pl.ds(0, CH)], load_sem.at[2]),
        pltpu.make_async_copy(v_hbm.at[pl.ds(CH, CH)], late.at[0, pl.ds(CH, CH)], load_sem.at[3]),
        pltpu.make_async_copy(q_hbm, q_in, load_sem.at[4]),
        pltpu.make_async_copy(w_hbm, w_in, load_sem.at[5]),
    ]
    for load in loads:
        load.start()

    def at(dy, dz, dc=0):
        y = ylo + dy - 2 * dy * ylo
        c = core + dc - 2 * dc * core
        return (y * 16 + lax.rem(z + dz + 8, 8) * 2 + c, inner)

    def along(d):
        return (blk, yhi * 4 + lax.rem(x + d + 4, 4))

    opposite = (blk, lax.rem(inner + 4, 8))
    barrier = pltpu.get_barrier_semaphore()
    greeted = [at(0, 1), at(0, -1), at(0, 2), at(0, -2), at(1, 0), at(0, 0, 1)]
    greeted += [along(1), along(-1), opposite]
    for device in greeted:
        pl.semaphore_signal(barrier, inc=1, device_id=device, device_id_type=MESH)

    sends = []

    def send(phase, src, dst, device):
        count = sum(1 for p, _ in sends if p == phase)
        copy = pltpu.make_async_remote_copy(
            src_ref=bufs[phase].at[src],
            dst_ref=bufs[phase].at[dst],
            send_sem=send_sem.at[phase, count],
            recv_sem=recv_sem.at[phase, dst],
            device_id=device,
            device_id_type=MESH,
        )
        copy.start()
        sends.append((phase, copy))

    def arrived(phase, slot):
        ref = bufs[phase].at[slot]
        pltpu.make_async_copy(ref, ref, recv_sem.at[phase, slot]).wait()

    def pass_on(phase, *chips):
        for chip in chips:
            slot = slot_of(chip)
            if chip != (0, 0):
                arrived(phase, slot)
            for to in TREES[phase].get(chip, ()):
                dz = (to[1] - chip[1] + 4) % 8 - 4
                send(phase, slot, slot_of(to), at(to[0] - chip[0], dz))
            send(phase, slot, slot + 1, at(0, 0, 1))

    def from_sibling(phase, group):
        for j in range(4 * group, 4 * group + 4):
            arrived(phase, 2 * j + 1)

    def attend(phase, which, group, first=False):
        buf = bufs[which]
        base = group * GROUP
        keys = buf[pl.ds(base, GROUP), pl.ds(0, CH), :].reshape(GROUP * CH, HEAD)
        values = buf[pl.ds(base, GROUP), pl.ds(CH, CH), :].reshape(GROUP * CH, HEAD)
        scores = jnp.dot(keys, q_t[phase], preferred_element_type=jnp.float32)
        if phase == which:
            tags = early[pl.ds(base, GROUP), pl.ds(2 * CH, 16), :].astype(jnp.float32)[:, :1, :]
            seen = tags < tag if phase == 0 else tags > tag
            bias = jnp.where(seen, 0.0, LOW)
            bias = jnp.concatenate([bias] * (LANES // HEAD), axis=2)
            scores = scores.reshape(GROUP, CH, LANES)
            if first:
                scores = jnp.concatenate([scores[:1] + tri[...][None], scores[1:] + bias[1:]], axis=0)
            else:
                scores = scores + bias
            scores = scores.reshape(GROUP * CH, LANES)
        old = high[phase]
        new = jnp.maximum(old, jnp.max(scores, axis=0, keepdims=True) * SCALE)
        weights = jnp.exp2(scores * SCALE - new)
        keep = jnp.exp2(old - new)
        high[phase] = new
        total[phase] = total[phase] * keep + jnp.sum(weights, axis=0, keepdims=True)
        mixed = lax.dot_general(
            values, weights.astype(jnp.bfloat16), (((0,), (0,)), ((), ())),
            preferred_element_type=jnp.float32,
        )
        acc[phase] = acc[phase] * keep + mixed

    def attend_many(phase, which, lo, hi):
        def body(group, carry):
            attend(phase, which, group)
            return carry

        lax.fori_loop(lo, hi, body, 0)

    row_sends = []

    def row_send_to(kind, phase, j, src, dst, device):
        copy = pltpu.make_async_remote_copy(
            src_ref=src, dst_ref=dst.at[phase, j],
            send_sem=row_send.at[kind, phase, j], recv_sem=row_recv.at[kind, phase, j],
            device_id=device, device_id_type=MESH,
        )
        return copy

    def row_wait(kind, phase, j, dst):
        ref = dst.at[phase, j]
        pltpu.make_async_copy(ref, ref, row_recv.at[kind, phase, j]).wait()

    def way(j):
        return 1 if j % 2 == 0 else -1

    def project(phase):
        rows = jnp.transpose(acc[phase] * (1.0 / total[phase])).astype(jnp.bfloat16)
        rows = jnp.concatenate([rows[h * CH : (h + 1) * CH] for h in range(PER_KEY)], axis=1)
        for piece in range(CHUNKS // 2):
            left, right = [
                jnp.dot(
                    rows, w_in[:, side * HALF + piece * 2 * WIDE : side * HALF + (piece + 1) * 2 * WIDE],
                    preferred_element_type=jnp.float32,
                )
                for side in range(2)
            ]
            for j in (2 * piece, 2 * piece + 1):
                cols = slice((j % 2) * WIDE, (j % 2 + 1) * WIDE)
                for d in range(4):
                    cut = slice(OWN * d, OWN * (d + 1))
                    both = jnp.concatenate([left[cut, cols], right[cut, cols]], axis=0)
                    part[phase, j, d] = both.astype(jnp.bfloat16)
            for j in (2 * piece, 2 * piece + 1):
                s = way(j)
                copy = row_send_to(0, phase, j, part.at[phase, j, lax.rem(x + 2, 4)], through, along(s))
                copy.start()
                row_sends.append(copy)
            for j in (2 * piece, 2 * piece + 1):
                s = way(j)
                copy = row_send_to(1, phase, j, part.at[phase, j, lax.rem(x + 4 - s, 4)], beside, along(-s))
                copy.start()
                row_sends.append(copy)

    def go_through(phase, *chunks):
        for j in chunks:
            s = way(j)
            row_wait(0, phase, j, through)
            mine = part[phase, j, lax.rem(x + 4 + s, 4)].astype(jnp.float32)
            through[phase, j] = (mine + through[phase, j].astype(jnp.float32)).astype(jnp.bfloat16)
            copy = row_send_to(2, phase, j, through.at[phase, j], passed, along(s))
            copy.start()
            row_sends.append(copy)

    def ring_sum(phase, j):
        row_wait(1, phase, j, beside)
        row_wait(2, phase, j, passed)
        summed = part[phase, j, x].astype(jnp.float32) + beside[phase, j].astype(jnp.float32)
        return summed + passed[phase, j].astype(jnp.float32)

    def cross_copy(phase, j):
        return row_send_to(3, phase, j, across.at[phase, j], crossed, opposite)

    def cross(phase, *chunks):
        @pl.when(yhi != phase)
        def _():
            for j in chunks:
                across[phase, j] = ring_sum(phase, j).astype(jnp.bfloat16)
                cross_copy(phase, j).start()

    def finish(phase):
        @pl.when(yhi == phase)
        def _():
            for j in range(CHUNKS):
                summed = ring_sum(phase, j)
                row_wait(3, phase, j, crossed)
                summed = (summed + crossed[phase, j].astype(jnp.float32)).astype(out_ref.dtype)
                out_ref[:, j * WIDE : (j + 1) * WIDE] = summed[:OWN]
                out_ref[:, HALF + j * WIDE : HALF + (j + 1) * WIDE] = summed[OWN:]

        @pl.when(yhi != phase)
        def _():
            for j in range(CHUNKS):
                cross_copy(phase, j).wait_send()

    lane = lax.broadcasted_iota(jnp.int32, (CH, LANES), 1)
    start = sum(jnp.where(lane >= CH * h, CH, 0) for h in range(1, PER_KEY + 1))
    row = lax.broadcasted_iota(jnp.int32, (CH, LANES), 0)
    tri[...] = jnp.where(row <= lane - start, 0.0, LOW)
    high[...] = jnp.full(high.shape, LOW, jnp.float32)
    total[...] = jnp.zeros(total.shape, jnp.float32)
    acc[...] = jnp.zeros(acc.shape, jnp.float32)

    pl.semaphore_wait(barrier, len(greeted))
    loads[0].wait()
    tag = pos_in[0].astype(jnp.float32)
    early[0, pl.ds(2 * CH, 16), :] = jnp.full((16, HEAD), tag, jnp.float32).astype(jnp.bfloat16)
    loads[1].wait()
    loads[2].wait()
    pass_on(0, (0, 0))
    loads[3].wait()
    loads[4].wait()
    pass_on(1, (0, 0))
    loads[5].wait()
    for phase in range(2):
        heads = [q_in[pl.ds(CH * phase, CH), pl.ds(HEAD * h, HEAD)] for h in range(PER_KEY)]
        pad = jnp.zeros((LANES - PER_KEY * CH, HEAD), jnp.bfloat16)
        q_t[phase] = jnp.transpose(jnp.concatenate(heads + [pad], axis=0))

    pass_on(0, (0, 2), (0, -2), (0, 1), (0, -1), (1, 0))
    pass_on(1, (0, 1), (0, -1), (1, 0))
    from_sibling(0, 0)
    attend(0, 0, 0, first=True)
    attend(1, 0, 0)
    pass_on(0, (1, 2), (1, -2), (1, 1), (1, -1))
    pass_on(1, (0, 2), (0, -2))
    from_sibling(0, 1)
    attend(0, 0, 1)
    pass_on(0, (0, 3), (0, -3), (0, 4))
    attend(1, 0, 1)
    pass_on(1, (1, 1), (1, -1))
    from_sibling(0, 2)
    attend(0, 0, 2)
    pass_on(1, (0, 3), (0, -3))
    pass_on(0, (1, 3), (1, -3), (1, 4))
    from_sibling(0, 3)
    attend(0, 0, 3)
    loads[6].wait()
    project(0)
    pass_on(1, (1, 2), (1, -2), (0, 4))
    attend(1, 0, 2)
    attend(1, 0, 3)
    pass_on(1, (1, 3), (1, -3))
    from_sibling(1, 0)
    attend(1, 1, 0, first=True)
    pass_on(1, (1, 4))
    go_through(0, 0, 1)
    from_sibling(1, 1)
    attend(1, 1, 1)
    go_through(0, 2, 3)
    for group in range(2, 4):
        from_sibling(1, group)
        attend(1, 1, group)
    project(1)
    cross(0, *range(CHUNKS))
    go_through(1, *range(CHUNKS))
    finish(0)
    cross(1, *range(CHUNKS))
    finish(1)
    for _, copy in sends:
        copy.wait_send()
    for copy in row_sends:
        copy.wait_send()


def shards(queries, keys, values, positions, out_weight):
    any_space = pl.BlockSpec(memory_space=pl.ANY)
    return pl.pallas_call(
        kernel,
        out_shape=jax.ShapeDtypeStruct((OWN, 2 * HALF), jnp.bfloat16),
        in_specs=[any_space] * 5,
        out_specs=pl.BlockSpec(memory_space=pltpu.VMEM),
        scratch_shapes=[
            pltpu.VMEM((2 * CH, PER_KEY * HEAD), jnp.bfloat16),
            pltpu.VMEM((PER_KEY * HEAD, 2 * HALF), jnp.bfloat16),
            pltpu.SMEM((2 * CH,), jnp.int32),
            pltpu.VMEM((32, ROWS[0], HEAD), jnp.bfloat16),
            pltpu.VMEM((32, ROWS[1], HEAD), jnp.bfloat16),
            pltpu.VMEM((2, HEAD, LANES), jnp.bfloat16),
            pltpu.VMEM((2, 1, LANES), jnp.float32),
            pltpu.VMEM((2, 1, LANES), jnp.float32),
            pltpu.VMEM((2, HEAD, LANES), jnp.float32),
            pltpu.VMEM((CH, LANES), jnp.float32),
            pltpu.VMEM((2, CHUNKS, 4, 2 * OWN, WIDE), jnp.bfloat16),
            *[pltpu.VMEM((2, CHUNKS, 2 * OWN, WIDE), jnp.bfloat16) for _ in range(5)],
            pltpu.SemaphoreType.DMA((7,)),
            pltpu.SemaphoreType.DMA((2, 32)),
            pltpu.SemaphoreType.DMA((2, 32)),
            pltpu.SemaphoreType.DMA((4, 2, CHUNKS)),
            pltpu.SemaphoreType.DMA((4, 2, CHUNKS)),
        ],
        compiler_params=pltpu.CompilerParams(
            collective_id=0, has_side_effects=True, vmem_limit_bytes=62 << 20
        ),
        cost_estimate=pl.CostEstimate(
            flops=4_000_000_000, bytes_accessed=10_000_000, transcendentals=5_000_000
        ),
    )(queries, keys, values, positions, out_weight)


def solution(mesh):
    placed = (P("blk", "inner"), P("blk", "inner"), P("blk", "inner"), P("blk"), P("inner", None))
    return jax.shard_map(
        shards, mesh=mesh, in_specs=placed, out_specs=P(("blk", "inner"), None), check_vma=False
    )
```

```python
import math

import jax
import jax.numpy as jnp
from jax import lax
from jax.experimental import pallas as pl
from jax.experimental.pallas import tpu as pltpu
from jax.sharding import PartitionSpec as P

MESH = pl.DeviceIdType.MESH
HEAD = 128
PER_KEY = 5
CH = 96
LANES = 512
SCALE = math.log2(math.e) / math.sqrt(HEAD)
LOW = -1e30

CHIPS = (
    [(0, 0), (0, -1), (1, 0), (0, 2), (0, -2), (1, -1), (1, 1), (0, 3), (1, 2), (1, -3), (1, -2), (0, -3), (0, 1), (0, 4), (1, 4), (1, 3)],
    [(0, 0), (0, -1), (1, 0), (0, 2), (1, -1), (0, 3), (1, -2), (0, 4), (1, 3), (0, 1), (0, -2), (1, -3), (0, -3), (1, 4), (1, 1), (1, 2)],
)
TREES = (
    {
        (0, 0): [(0, -1), (0, 2), (1, 0)],
        (0, -1): [(0, -2), (1, -1)],
        (1, 0): [(1, 1), (1, -3)],
        (0, 2): [(0, 3), (1, 2)],
        (0, -2): [(0, -3), (1, -2)],
        (1, 1): [(0, 1)],
        (0, 3): [(0, 4), (1, 3)],
        (1, -3): [(1, 4)],
    },
    {
        (0, 0): [(0, -1), (0, 2), (1, 0)],
        (0, -1): [(1, -1)],
        (0, 2): [(0, 3)],
        (1, -1): [(1, -2)],
        (0, 3): [(0, 4), (1, 3), (0, 1)],
        (1, -2): [(0, -2), (1, 1), (1, -3)],
        (0, 4): [(0, -3), (1, 4)],
        (1, 3): [(1, 2)],
    },
)
PLAN = [
    ("take", 0, (0, -1), (1, 0)),
    ("take", 1, (0, -1), (1, 0)),
    ("take", 0, (0, 2)),
    ("take", 1, (0, 2)),
    ("take", 0, (0, -2), (1, -1), (1, 1)),
    ("attend", 0, 0, 0),
    ("take", 1, (1, -1)),
    ("attend", 1, 1, 0),
    ("take", 0, (0, 3), (1, 2), (1, -3)),
    ("attend", 1, 0, 0),
    ("take", 1, (0, 3)),
    ("take", 0, (1, -2), (0, -3)),
    ("attend", 0, 0, 1),
    ("take", 1, (1, -2)),
    ("take", 0, (0, 1), (0, 4)),
    ("attend", 0, 0, 2),
    ("take", 0, (1, 4), (1, 3)),
    ("take", 1, (0, 4)),
    ("attend", 1, 0, 1),
    ("take", 1, (1, 3), (0, 1)),
    ("attend", 0, 0, 3),
    ("take", 1, (0, -2), (1, -3)),
    ("project", 0),
    ("take", 1, (0, -3), (1, 4), (1, 1), (1, 2)),
    ("attend", 1, 1, 1),
    ("attend", 1, 1, 2),
    ("attend", 1, 1, 3),
    ("attend", 1, 0, 2),
    ("through", 0, 0, 1),
    ("attend", 1, 0, 3),
    ("through", 0, 2, 3),
    ("cross", 0, 0, 1, 2, 3),
    ("project", 1),
]
SLOT = tuple({chip: 2 * j for j, chip in enumerate(chips)} for chips in CHIPS)
GROUP = 8
ROWS = (208, 208)
OWN = 24
HALF = 2560
CHUNKS = 4
WIDE = HALF // CHUNKS


def step(chip, to):
    return abs(to[0] - chip[0]), (to[1] - chip[1] + 3) % 8 - 3


def kernel(
    q_hbm, k_hbm, v_hbm, pos_hbm, w_hbm, out_ref,
    q_in, w_in, pos_in, early, late, q_t, high, total, acc, tri,
    part, through, passed, beside, across, crossed,
    load_sem, send_sem, recv_sem, row_send, row_recv,
):
    blk, inner = lax.axis_index("blk"), lax.axis_index("inner")
    ylo, z, core = blk // 16, (blk // 2) % 8, blk % 2
    yhi, x = inner // 4, inner % 4
    bufs = (early, late)

    loads = [
        pltpu.make_async_copy(pos_hbm, pos_in, load_sem.at[6]),
        pltpu.make_async_copy(k_hbm.at[pl.ds(0, CH)], early.at[0, pl.ds(0, CH)], load_sem.at[0]),
        pltpu.make_async_copy(v_hbm.at[pl.ds(0, CH)], early.at[0, pl.ds(CH, CH)], load_sem.at[1]),
        pltpu.make_async_copy(k_hbm.at[pl.ds(CH, CH)], late.at[0, pl.ds(0, CH)], load_sem.at[2]),
        pltpu.make_async_copy(v_hbm.at[pl.ds(CH, CH)], late.at[0, pl.ds(CH, CH)], load_sem.at[3]),
        pltpu.make_async_copy(q_hbm, q_in, load_sem.at[4]),
        pltpu.make_async_copy(w_hbm, w_in, load_sem.at[5]),
    ]
    for load in loads:
        load.start()

    def at(dy, dz, dc=0):
        y = ylo + dy - 2 * dy * ylo
        c = core + dc - 2 * dc * core
        return (y * 16 + lax.rem(z + dz * (1 - 2 * core) + 8, 8) * 2 + c, inner)

    def along(d):
        return (blk, yhi * 4 + lax.rem(x + d + 4, 4))

    opposite = (blk, lax.rem(inner + 4, 8))
    barrier = pltpu.get_barrier_semaphore()
    steps = {step(a, b)[1] for tree in TREES for a, ends in tree.items() for b in ends}
    steps = sorted({d % 8 for d in steps if d} | {-d % 8 for d in steps if d})
    greeted = [at(0, d) for d in steps] + [at(1, 0), at(0, 0, 1)]
    greeted += [along(1), along(-1), opposite]
    for device in greeted:
        pl.semaphore_signal(barrier, inc=1, device_id=device, device_id_type=MESH)

    sends = []

    def send(phase, src, dst, device):
        count = sum(1 for p, _ in sends if p == phase)
        copy = pltpu.make_async_remote_copy(
            src_ref=bufs[phase].at[src],
            dst_ref=bufs[phase].at[dst],
            send_sem=send_sem.at[phase, count],
            recv_sem=recv_sem.at[phase, dst],
            device_id=device,
            device_id_type=MESH,
        )
        copy.start()
        sends.append((phase, copy))

    def arrived(phase, slot):
        ref = bufs[phase].at[slot]
        pltpu.make_async_copy(ref, ref, recv_sem.at[phase, slot]).wait()

    def pass_on(phase, *chips):
        for chip in chips:
            slot = SLOT[phase][chip]
            if chip != (0, 0):
                arrived(phase, slot)
            for to in TREES[phase].get(chip, ()):
                send(phase, slot, SLOT[phase][to], at(*step(chip, to)))
            send(phase, slot, slot + 1, at(0, 0, 1))

    taken = set()

    def from_sibling_once(phase, group):
        if (phase, group) in taken:
            return
        taken.add((phase, group))
        for j in range(4 * group, 4 * group + 4):
            arrived(phase, 2 * j + 1)

    def attend(phase, which, group, first=False):
        buf = bufs[which]
        base = group * GROUP
        keys = buf[pl.ds(base, GROUP), pl.ds(0, CH), :].reshape(GROUP * CH, HEAD)
        values = buf[pl.ds(base, GROUP), pl.ds(CH, CH), :].reshape(GROUP * CH, HEAD)
        scores = jnp.dot(keys, q_t[phase], preferred_element_type=jnp.float32)
        if phase == which:
            tags = buf[pl.ds(base, GROUP), pl.ds(2 * CH, 16), :].astype(jnp.float32)[:, :1, :]
            seen = tags < tag if phase == 0 else tags > tag
            bias = jnp.where(seen, 0.0, LOW)
            bias = jnp.concatenate([bias] * (LANES // HEAD), axis=2)
            scores = scores.reshape(GROUP, CH, LANES)
            if first:
                scores = jnp.concatenate([scores[:1] + tri[...][None], scores[1:] + bias[1:]], axis=0)
            else:
                scores = scores + bias
            scores = scores.reshape(GROUP * CH, LANES)
        old = high[phase]
        new = jnp.maximum(old, jnp.max(scores, axis=0, keepdims=True) * SCALE)
        weights = jnp.exp2(scores * SCALE - new)
        keep = jnp.exp2(old - new)
        high[phase] = new
        total[phase] = total[phase] * keep + jnp.sum(weights, axis=0, keepdims=True)
        mixed = lax.dot_general(
            values, weights.astype(jnp.bfloat16), (((0,), (0,)), ((), ())),
            preferred_element_type=jnp.float32,
        )
        acc[phase] = acc[phase] * keep + mixed

    row_sends = []

    def row_send_to(kind, phase, j, src, dst, device):
        copy = pltpu.make_async_remote_copy(
            src_ref=src, dst_ref=dst.at[phase, j],
            send_sem=row_send.at[kind, phase, j], recv_sem=row_recv.at[kind, phase, j],
            device_id=device, device_id_type=MESH,
        )
        return copy

    def row_wait(kind, phase, j, dst):
        ref = dst.at[phase, j]
        pltpu.make_async_copy(ref, ref, row_recv.at[kind, phase, j]).wait()

    def way(j):
        return 1 if j % 2 == 0 else -1

    def project(phase):
        if phase == 0:
            loads[6].wait()
        rows = jnp.transpose(acc[phase] * (1.0 / total[phase])).astype(jnp.bfloat16)
        rows = jnp.concatenate([rows[h * CH : (h + 1) * CH] for h in range(PER_KEY)], axis=1)
        for piece in range(CHUNKS // 2):
            left, right = [
                jnp.dot(
                    rows, w_in[:, side * HALF + piece * 2 * WIDE : side * HALF + (piece + 1) * 2 * WIDE],
                    preferred_element_type=jnp.float32,
                )
                for side in range(2)
            ]
            for j in (2 * piece, 2 * piece + 1):
                cols = slice((j % 2) * WIDE, (j % 2 + 1) * WIDE)
                for d in range(4):
                    cut = slice(OWN * d, OWN * (d + 1))
                    both = jnp.concatenate([left[cut, cols], right[cut, cols]], axis=0)
                    part[phase, j, d] = both.astype(jnp.bfloat16)
            for j in (2 * piece, 2 * piece + 1):
                s = way(j)
                copy = row_send_to(0, phase, j, part.at[phase, j, lax.rem(x + 2, 4)], through, along(s))
                copy.start()
                row_sends.append(copy)
            for j in (2 * piece, 2 * piece + 1):
                s = way(j)
                copy = row_send_to(1, phase, j, part.at[phase, j, lax.rem(x + 4 - s, 4)], beside, along(-s))
                copy.start()
                row_sends.append(copy)

    def go_through(phase, *chunks):
        for j in chunks:
            s = way(j)
            row_wait(0, phase, j, through)
            mine = part[phase, j, lax.rem(x + 4 + s, 4)].astype(jnp.float32)
            through[phase, j] = (mine + through[phase, j].astype(jnp.float32)).astype(jnp.bfloat16)
            copy = row_send_to(2, phase, j, through.at[phase, j], passed, along(s))
            copy.start()
            row_sends.append(copy)

    def ring_sum(phase, j):
        row_wait(1, phase, j, beside)
        row_wait(2, phase, j, passed)
        summed = part[phase, j, x].astype(jnp.float32) + beside[phase, j].astype(jnp.float32)
        return summed + passed[phase, j].astype(jnp.float32)

    def cross_copy(phase, j):
        return row_send_to(3, phase, j, across.at[phase, j], crossed, opposite)

    def cross(phase, *chunks):
        @pl.when(yhi != phase)
        def _():
            for j in chunks:
                across[phase, j] = ring_sum(phase, j).astype(jnp.bfloat16)
                cross_copy(phase, j).start()

    def finish(phase):
        @pl.when(yhi == phase)
        def _():
            for j in range(CHUNKS):
                summed = ring_sum(phase, j)
                row_wait(3, phase, j, crossed)
                summed = (summed + crossed[phase, j].astype(jnp.float32)).astype(out_ref.dtype)
                out_ref[:, j * WIDE : (j + 1) * WIDE] = summed[:OWN]
                out_ref[:, HALF + j * WIDE : HALF + (j + 1) * WIDE] = summed[OWN:]

        @pl.when(yhi != phase)
        def _():
            for j in range(CHUNKS):
                cross_copy(phase, j).wait_send()

    lane = lax.broadcasted_iota(jnp.int32, (CH, LANES), 1)
    start = sum(jnp.where(lane >= CH * h, CH, 0) for h in range(1, PER_KEY + 1))
    row = lax.broadcasted_iota(jnp.int32, (CH, LANES), 0)
    tri[...] = jnp.where(row <= lane - start, 0.0, LOW)
    high[...] = jnp.full(high.shape, LOW, jnp.float32)
    total[...] = jnp.zeros(total.shape, jnp.float32)
    acc[...] = jnp.zeros(acc.shape, jnp.float32)

    pl.semaphore_wait(barrier, len(greeted))
    loads[0].wait()
    tag = pos_in[0].astype(jnp.float32)
    for buf in bufs:
        buf[0, pl.ds(2 * CH, 16), :] = jnp.full((16, HEAD), tag, jnp.float32).astype(jnp.bfloat16)
    loads[1].wait()
    loads[2].wait()
    pass_on(0, (0, 0))
    loads[3].wait()
    loads[4].wait()
    pass_on(1, (0, 0))
    loads[5].wait()
    for phase in range(2):
        heads = [q_in[pl.ds(CH * phase, CH), pl.ds(HEAD * h, HEAD)] for h in range(PER_KEY)]
        pad = jnp.zeros((LANES - PER_KEY * CH, HEAD), jnp.bfloat16)
        q_t[phase] = jnp.transpose(jnp.concatenate(heads + [pad], axis=0))

    for what, *which in PLAN:
        if what == "take":
            pass_on(*which)
        elif what == "attend":
            phase, side, group = which
            from_sibling_once(side, group)
            attend(phase, side, group, first=phase == side and group == 0)
        elif what == "project":
            project(*which)
        elif what == "cross":
            cross(*which)
        elif what == "through":
            go_through(*which)
    go_through(1, 0, 1)
    go_through(1, 2, 3)
    cross(1, *range(CHUNKS))
    finish(0)
    finish(1)
    for _, copy in sends:
        copy.wait_send()
    for copy in row_sends:
        copy.wait_send()


def shards(queries, keys, values, positions, out_weight):
    any_space = pl.BlockSpec(memory_space=pl.ANY)
    return pl.pallas_call(
        kernel,
        out_shape=jax.ShapeDtypeStruct((OWN, 2 * HALF), jnp.bfloat16),
        in_specs=[any_space] * 5,
        out_specs=pl.BlockSpec(memory_space=pltpu.VMEM),
        scratch_shapes=[
            pltpu.VMEM((2 * CH, PER_KEY * HEAD), jnp.bfloat16),
            pltpu.VMEM((PER_KEY * HEAD, 2 * HALF), jnp.bfloat16),
            pltpu.SMEM((2 * CH,), jnp.int32),
            pltpu.VMEM((32, ROWS[0], HEAD), jnp.bfloat16),
            pltpu.VMEM((32, ROWS[1], HEAD), jnp.bfloat16),
            pltpu.VMEM((2, HEAD, LANES), jnp.bfloat16),
            pltpu.VMEM((2, 1, LANES), jnp.float32),
            pltpu.VMEM((2, 1, LANES), jnp.float32),
            pltpu.VMEM((2, HEAD, LANES), jnp.float32),
            pltpu.VMEM((CH, LANES), jnp.float32),
            pltpu.VMEM((2, CHUNKS, 4, 2 * OWN, WIDE), jnp.bfloat16),
            *[pltpu.VMEM((2, CHUNKS, 2 * OWN, WIDE), jnp.bfloat16) for _ in range(5)],
            pltpu.SemaphoreType.DMA((7,)),
            pltpu.SemaphoreType.DMA((2, 32)),
            pltpu.SemaphoreType.DMA((2, 32)),
            pltpu.SemaphoreType.DMA((4, 2, CHUNKS)),
            pltpu.SemaphoreType.DMA((4, 2, CHUNKS)),
        ],
        compiler_params=pltpu.CompilerParams(
            collective_id=0, has_side_effects=True, vmem_limit_bytes=62 << 20
        ),
        cost_estimate=pl.CostEstimate(
            flops=4_000_000_000, bytes_accessed=10_000_000, transcendentals=5_000_000
        ),
    )(queries, keys, values, positions, out_weight)


def solution(mesh):
    placed = (P("blk", "inner"), P("blk", "inner"), P("blk", "inner"), P("blk"), P("inner", None))
    return jax.shard_map(
        shards, mesh=mesh, in_specs=placed, out_specs=P(("blk", "inner"), None), check_vma=False
    )
```

```python
import math

import jax
import jax.numpy as jnp
from jax import lax
from jax.experimental import pallas as pl
from jax.experimental.pallas import tpu as pltpu
from jax.sharding import PartitionSpec as P

MESH = pl.DeviceIdType.MESH
HEAD = 128
PER_KEY = 5
CH = 96
LANES = 512
SCALE = math.log2(math.e) / math.sqrt(HEAD)
LOW = -1e30

CHIPS = (
    [(0, 0), (0, -1), (1, 0), (0, 2), (0, -2), (1, -1), (1, 1), (0, 3), (1, 2), (1, -3), (1, -2), (0, -3), (0, 1), (0, 4), (1, 4), (1, 3)],
    [(0, 0), (0, -1), (1, 0), (0, 2), (1, -1), (0, 3), (1, -2), (0, 4), (1, 3), (0, 1), (0, -2), (1, -3), (0, -3), (1, 4), (1, 1), (1, 2)],
)
TREES = (
    {
        (0, 0): [(0, -1), (0, 2), (1, 0)],
        (0, -1): [(0, -2), (1, -1)],
        (1, 0): [(1, 1), (1, -3)],
        (0, 2): [(0, 3), (1, 2)],
        (0, -2): [(0, -3), (1, -2)],
        (1, 1): [(0, 1)],
        (0, 3): [(0, 4), (1, 3)],
        (1, -3): [(1, 4)],
    },
    {
        (0, 0): [(0, -1), (0, 2), (1, 0)],
        (0, -1): [(1, -1)],
        (0, 2): [(0, 3)],
        (1, -1): [(1, -2)],
        (0, 3): [(0, 4), (1, 3), (0, 1)],
        (1, -2): [(0, -2), (1, 1), (1, -3)],
        (0, 4): [(0, -3), (1, 4)],
        (1, 3): [(1, 2)],
    },
)
PLAN = [
    ("take", 0, (0, -1), (1, 0)),
    ("take", 1, (0, -1), (1, 0)),
    ("take", 0, (0, 2)),
    ("take", 1, (0, 2)),
    ("take", 0, (0, -2), (1, -1), (1, 1)),
    ("attend", 0, 0, 0),
    ("take", 1, (1, -1)),
    ("attend", 1, 1, 0),
    ("take", 0, (0, 3), (1, 2), (1, -3)),
    ("attend", 1, 0, 0),
    ("take", 1, (0, 3)),
    ("take", 0, (1, -2), (0, -3)),
    ("attend", 0, 0, 1),
    ("take", 1, (1, -2)),
    ("take", 0, (0, 1), (0, 4)),
    ("attend", 0, 0, 2),
    ("take", 0, (1, 4), (1, 3)),
    ("take", 1, (0, 4)),
    ("attend", 1, 0, 1),
    ("take", 1, (1, 3), (0, 1)),
    ("attend", 0, 0, 3),
    ("take", 1, (0, -2), (1, -3)),
    ("project", 0),
    ("attend", 1, 0, 2),
    ("attend", 1, 0, 3),
    ("take", 1, (0, -3), (1, 4), (1, 1), (1, 2)),
    ("attend", 1, 1, 1),
    ("through", 0, 0, 1, 2, 3),
    ("attend", 1, 1, 2),
    ("attend", 1, 1, 3),
    ("cross", 0, 0, 1, 2, 3),
    ("project", 1),
]
SLOT = tuple({chip: 2 * j for j, chip in enumerate(chips)} for chips in CHIPS)
GROUP = 8
ROWS = (208, 208)
OWN = 24
HALF = 2560
CHUNKS = 4
WIDE = HALF // CHUNKS


def step(chip, to):
    return abs(to[0] - chip[0]), (to[1] - chip[1] + 3) % 8 - 3


def kernel(
    q_hbm, k_hbm, v_hbm, pos_hbm, w_hbm, out_ref,
    q_in, w_in, pos_in, early, late, q_t, high, total, acc, tri,
    part, through, passed, beside, across, crossed,
    load_sem, send_sem, recv_sem, row_send, row_recv,
):
    blk, inner = lax.axis_index("blk"), lax.axis_index("inner")
    ylo, z, core = blk // 16, (blk // 2) % 8, blk % 2
    yhi, x = inner // 4, inner % 4
    bufs = (early, late)

    loads = [
        pltpu.make_async_copy(pos_hbm, pos_in, load_sem.at[6]),
        pltpu.make_async_copy(k_hbm.at[pl.ds(0, CH)], early.at[0, pl.ds(0, CH)], load_sem.at[0]),
        pltpu.make_async_copy(v_hbm.at[pl.ds(0, CH)], early.at[0, pl.ds(CH, CH)], load_sem.at[1]),
        pltpu.make_async_copy(k_hbm.at[pl.ds(CH, CH)], late.at[0, pl.ds(0, CH)], load_sem.at[2]),
        pltpu.make_async_copy(v_hbm.at[pl.ds(CH, CH)], late.at[0, pl.ds(CH, CH)], load_sem.at[3]),
        pltpu.make_async_copy(q_hbm, q_in, load_sem.at[4]),
        pltpu.make_async_copy(w_hbm, w_in, load_sem.at[5]),
    ]
    for load in loads:
        load.start()

    def at(dy, dz, dc=0):
        y = ylo + dy - 2 * dy * ylo
        c = core + dc - 2 * dc * core
        return (y * 16 + lax.rem(z + dz * (1 - 2 * core) + 8, 8) * 2 + c, inner)

    def along(d):
        return (blk, yhi * 4 + lax.rem(x + d + 4, 4))

    opposite = (blk, lax.rem(inner + 4, 8))
    barrier = pltpu.get_barrier_semaphore()
    steps = {step(a, b)[1] for tree in TREES for a, ends in tree.items() for b in ends}
    steps = sorted({d % 8 for d in steps if d} | {-d % 8 for d in steps if d})
    greeted = [at(0, d) for d in steps] + [at(1, 0), at(0, 0, 1)]
    greeted += [along(1), along(-1), opposite]
    for device in greeted:
        pl.semaphore_signal(barrier, inc=1, device_id=device, device_id_type=MESH)

    sends = []

    def send(phase, src, dst, device):
        count = sum(1 for p, _ in sends if p == phase)
        copy = pltpu.make_async_remote_copy(
            src_ref=bufs[phase].at[src],
            dst_ref=bufs[phase].at[dst],
            send_sem=send_sem.at[phase, count],
            recv_sem=recv_sem.at[phase, dst],
            device_id=device,
            device_id_type=MESH,
        )
        copy.start()
        sends.append((phase, copy))

    def arrived(phase, slot):
        ref = bufs[phase].at[slot]
        pltpu.make_async_copy(ref, ref, recv_sem.at[phase, slot]).wait()

    def pass_on(phase, *chips):
        for chip in chips:
            slot = SLOT[phase][chip]
            if chip != (0, 0):
                arrived(phase, slot)
            for to in TREES[phase].get(chip, ()):
                send(phase, slot, SLOT[phase][to], at(*step(chip, to)))
            send(phase, slot, slot + 1, at(0, 0, 1))

    taken = set()

    def from_sibling_once(phase, group):
        if (phase, group) in taken:
            return
        taken.add((phase, group))
        for j in range(4 * group, 4 * group + 4):
            arrived(phase, 2 * j + 1)

    def attend(phase, which, group, first=False):
        buf = bufs[which]
        base = group * GROUP
        keys = buf[pl.ds(base, GROUP), pl.ds(0, CH), :].reshape(GROUP * CH, HEAD)
        values = buf[pl.ds(base, GROUP), pl.ds(CH, CH), :].reshape(GROUP * CH, HEAD)
        scores = jnp.dot(keys, q_t[phase], preferred_element_type=jnp.float32)
        if phase == which:
            tags = buf[pl.ds(base, GROUP), pl.ds(2 * CH, 16), :].astype(jnp.float32)[:, :1, :]
            seen = tags < tag if phase == 0 else tags > tag
            bias = jnp.where(seen, 0.0, LOW)
            bias = jnp.concatenate([bias] * (LANES // HEAD), axis=2)
            scores = scores.reshape(GROUP, CH, LANES)
            if first:
                scores = jnp.concatenate([scores[:1] + tri[...][None], scores[1:] + bias[1:]], axis=0)
            else:
                scores = scores + bias
            scores = scores.reshape(GROUP * CH, LANES)
        old = high[phase]
        new = jnp.maximum(old, jnp.max(scores, axis=0, keepdims=True) * SCALE)
        weights = jnp.exp2(scores * SCALE - new)
        keep = jnp.exp2(old - new)
        high[phase] = new
        total[phase] = total[phase] * keep + jnp.sum(weights, axis=0, keepdims=True)
        mixed = lax.dot_general(
            values, weights.astype(jnp.bfloat16), (((0,), (0,)), ((), ())),
            preferred_element_type=jnp.float32,
        )
        acc[phase] = acc[phase] * keep + mixed

    row_sends = []

    def row_send_to(kind, phase, j, src, dst, device):
        copy = pltpu.make_async_remote_copy(
            src_ref=src, dst_ref=dst.at[phase, j],
            send_sem=row_send.at[kind, phase, j], recv_sem=row_recv.at[kind, phase, j],
            device_id=device, device_id_type=MESH,
        )
        return copy

    def row_wait(kind, phase, j, dst):
        ref = dst.at[phase, j]
        pltpu.make_async_copy(ref, ref, row_recv.at[kind, phase, j]).wait()

    def way(j):
        return 1 if j % 2 == 0 else -1

    def project(phase):
        if phase == 0:
            loads[6].wait()
        rows = jnp.transpose(acc[phase] * (1.0 / total[phase])).astype(jnp.bfloat16)
        rows = jnp.concatenate([rows[h * CH : (h + 1) * CH] for h in range(PER_KEY)], axis=1)
        for piece in range(CHUNKS // 2):
            left, right = [
                jnp.dot(
                    rows, w_in[:, side * HALF + piece * 2 * WIDE : side * HALF + (piece + 1) * 2 * WIDE],
                    preferred_element_type=jnp.float32,
                )
                for side in range(2)
            ]
            for j in (2 * piece, 2 * piece + 1):
                cols = slice((j % 2) * WIDE, (j % 2 + 1) * WIDE)
                for d in range(4):
                    cut = slice(OWN * d, OWN * (d + 1))
                    both = jnp.concatenate([left[cut, cols], right[cut, cols]], axis=0)
                    part[phase, j, d] = both.astype(jnp.bfloat16)
            for j in (2 * piece, 2 * piece + 1):
                s = way(j)
                copy = row_send_to(0, phase, j, part.at[phase, j, lax.rem(x + 2, 4)], through, along(s))
                copy.start()
                row_sends.append(copy)
            for j in (2 * piece, 2 * piece + 1):
                s = way(j)
                copy = row_send_to(1, phase, j, part.at[phase, j, lax.rem(x + 4 - s, 4)], beside, along(-s))
                copy.start()
                row_sends.append(copy)

    def go_through(phase, *chunks):
        for j in chunks:
            s = way(j)
            row_wait(0, phase, j, through)
            mine = part[phase, j, lax.rem(x + 4 + s, 4)].astype(jnp.float32)
            through[phase, j] = (mine + through[phase, j].astype(jnp.float32)).astype(jnp.bfloat16)
            copy = row_send_to(2, phase, j, through.at[phase, j], passed, along(s))
            copy.start()
            row_sends.append(copy)

    def ring_sum(phase, j):
        row_wait(1, phase, j, beside)
        row_wait(2, phase, j, passed)
        summed = part[phase, j, x].astype(jnp.float32) + beside[phase, j].astype(jnp.float32)
        return summed + passed[phase, j].astype(jnp.float32)

    def cross_copy(phase, j):
        return row_send_to(3, phase, j, across.at[phase, j], crossed, opposite)

    def cross(phase, *chunks):
        @pl.when(yhi != phase)
        def _():
            for j in chunks:
                across[phase, j] = ring_sum(phase, j).astype(jnp.bfloat16)
                cross_copy(phase, j).start()

    def finish(phase):
        @pl.when(yhi == phase)
        def _():
            for j in range(CHUNKS):
                summed = ring_sum(phase, j)
                row_wait(3, phase, j, crossed)
                summed = (summed + crossed[phase, j].astype(jnp.float32)).astype(out_ref.dtype)
                out_ref[:, j * WIDE : (j + 1) * WIDE] = summed[:OWN]
                out_ref[:, HALF + j * WIDE : HALF + (j + 1) * WIDE] = summed[OWN:]

        @pl.when(yhi != phase)
        def _():
            for j in range(CHUNKS):
                cross_copy(phase, j).wait_send()

    lane = lax.broadcasted_iota(jnp.int32, (CH, LANES), 1)
    start = sum(jnp.where(lane >= CH * h, CH, 0) for h in range(1, PER_KEY + 1))
    row = lax.broadcasted_iota(jnp.int32, (CH, LANES), 0)
    tri[...] = jnp.where(row <= lane - start, 0.0, LOW)
    high[...] = jnp.full(high.shape, LOW, jnp.float32)
    total[...] = jnp.zeros(total.shape, jnp.float32)
    acc[...] = jnp.zeros(acc.shape, jnp.float32)

    pl.semaphore_wait(barrier, len(greeted))
    loads[0].wait()
    tag = pos_in[0].astype(jnp.float32)
    for buf in bufs:
        buf[0, pl.ds(2 * CH, 16), :] = jnp.full((16, HEAD), tag, jnp.float32).astype(jnp.bfloat16)
    loads[1].wait()
    loads[2].wait()
    pass_on(0, (0, 0))
    loads[3].wait()
    loads[4].wait()
    pass_on(1, (0, 0))
    loads[5].wait()
    for phase in range(2):
        heads = [q_in[pl.ds(CH * phase, CH), pl.ds(HEAD * h, HEAD)] for h in range(PER_KEY)]
        pad = jnp.zeros((LANES - PER_KEY * CH, HEAD), jnp.bfloat16)
        q_t[phase] = jnp.transpose(jnp.concatenate(heads + [pad], axis=0))

    for what, *which in PLAN:
        if what == "take":
            pass_on(*which)
        elif what == "attend":
            phase, side, group = which
            from_sibling_once(side, group)
            attend(phase, side, group, first=phase == side and group == 0)
        elif what == "project":
            project(*which)
        elif what == "cross":
            cross(*which)
        elif what == "through":
            go_through(*which)
    go_through(1, 0, 1)
    go_through(1, 2, 3)
    cross(1, *range(CHUNKS))
    finish(0)
    finish(1)
    for _, copy in sends:
        copy.wait_send()
    for copy in row_sends:
        copy.wait_send()


def shards(queries, keys, values, positions, out_weight):
    any_space = pl.BlockSpec(memory_space=pl.ANY)
    return pl.pallas_call(
        kernel,
        out_shape=jax.ShapeDtypeStruct((OWN, 2 * HALF), jnp.bfloat16),
        in_specs=[any_space] * 5,
        out_specs=pl.BlockSpec(memory_space=pltpu.VMEM),
        scratch_shapes=[
            pltpu.VMEM((2 * CH, PER_KEY * HEAD), jnp.bfloat16),
            pltpu.VMEM((PER_KEY * HEAD, 2 * HALF), jnp.bfloat16),
            pltpu.SMEM((2 * CH,), jnp.int32),
            pltpu.VMEM((32, ROWS[0], HEAD), jnp.bfloat16),
            pltpu.VMEM((32, ROWS[1], HEAD), jnp.bfloat16),
            pltpu.VMEM((2, HEAD, LANES), jnp.bfloat16),
            pltpu.VMEM((2, 1, LANES), jnp.float32),
            pltpu.VMEM((2, 1, LANES), jnp.float32),
            pltpu.VMEM((2, HEAD, LANES), jnp.float32),
            pltpu.VMEM((CH, LANES), jnp.float32),
            pltpu.VMEM((2, CHUNKS, 4, 2 * OWN, WIDE), jnp.bfloat16),
            *[pltpu.VMEM((2, CHUNKS, 2 * OWN, WIDE), jnp.bfloat16) for _ in range(5)],
            pltpu.SemaphoreType.DMA((7,)),
            pltpu.SemaphoreType.DMA((2, 32)),
            pltpu.SemaphoreType.DMA((2, 32)),
            pltpu.SemaphoreType.DMA((4, 2, CHUNKS)),
            pltpu.SemaphoreType.DMA((4, 2, CHUNKS)),
        ],
        compiler_params=pltpu.CompilerParams(
            collective_id=0, has_side_effects=True, vmem_limit_bytes=62 << 20
        ),
        cost_estimate=pl.CostEstimate(
            flops=4_000_000_000, bytes_accessed=10_000_000, transcendentals=5_000_000
        ),
    )(queries, keys, values, positions, out_weight)


def solution(mesh):
    placed = (P("blk", "inner"), P("blk", "inner"), P("blk", "inner"), P("blk"), P("inner", None))
    return jax.shard_map(
        shards, mesh=mesh, in_specs=placed, out_specs=P(("blk", "inner"), None), check_vma=False
    )
```

```python
import math

import jax
import jax.numpy as jnp
from jax import lax
from jax.experimental import pallas as pl
from jax.experimental.pallas import tpu as pltpu
from jax.sharding import PartitionSpec as P

MESH = pl.DeviceIdType.MESH
HEAD = 128
PER_KEY = 5
CH = 96
LANES = 512
SCALE = math.log2(math.e) / math.sqrt(HEAD)
LOW = -1e30

CHIPS = (
    [(0, 0), (0, -1), (1, 0), (0, 2), (0, -2), (1, -1), (1, 1), (0, 3), (1, 2), (1, -3), (1, -2), (0, -3), (0, 1), (0, 4), (1, 4), (1, 3)],
    [(0, 0), (0, -1), (1, 0), (0, 2), (1, -1), (0, 3), (1, -2), (0, 4), (1, 3), (0, 1), (0, -2), (1, -3), (0, -3), (1, 4), (1, 1), (1, 2)],
)
TREES = (
    {
        (0, 0): [(0, -1), (0, 2), (1, 0)],
        (0, -1): [(0, -2), (1, -1)],
        (1, 0): [(1, 1), (1, -3)],
        (0, 2): [(0, 3), (1, 2)],
        (0, -2): [(0, -3), (1, -2)],
        (1, 1): [(0, 1)],
        (0, 3): [(0, 4), (1, 3)],
        (1, -3): [(1, 4)],
    },
    {
        (0, 0): [(0, -1), (0, 2), (1, 0)],
        (0, -1): [(1, -1)],
        (0, 2): [(0, 3)],
        (1, -1): [(1, -2)],
        (0, 3): [(0, 4), (1, 3), (0, 1)],
        (1, -2): [(0, -2), (1, 1), (1, -3)],
        (0, 4): [(0, -3), (1, 4)],
        (1, 3): [(1, 2)],
    },
)
PLAN = [
    ("take", 0, (0, -1), (1, 0)),
    ("take", 1, (0, -1), (1, 0)),
    ("take", 0, (0, 2)),
    ("take", 1, (0, 2)),
    ("take", 0, (0, -2), (1, -1), (1, 1)),
    ("attend", 0, 0, 0),
    ("take", 1, (1, -1)),
    ("attend", 1, 1, 0),
    ("take", 0, (0, 3), (1, 2), (1, -3)),
    ("attend", 1, 0, 0),
    ("take", 1, (0, 3)),
    ("take", 0, (1, -2), (0, -3)),
    ("attend", 0, 0, 1),
    ("take", 1, (1, -2)),
    ("take", 0, (0, 1), (0, 4)),
    ("attend", 0, 0, 2),
    ("take", 0, (1, 4), (1, 3)),
    ("take", 1, (0, 4)),
    ("attend", 1, 0, 1),
    ("take", 1, (1, 3), (0, 1)),
    ("attend", 1, 1, 1),
    ("attend", 0, 0, 3),
    ("take", 1, (0, -2), (1, -3)),
    ("project", 0),
    ("take", 1, (0, -3), (1, 4), (1, 1), (1, 2)),
    ("attend", 1, 1, 2),
    ("attend", 1, 1, 3),
    ("attend", 1, 0, 2),
    ("through", 0, 0, 1),
    ("attend", 1, 0, 3),
    ("through", 0, 2, 3),
    ("cross", 0, 0, 1, 2, 3),
    ("project", 1),
]
SLOT = tuple({chip: 2 * j for j, chip in enumerate(chips)} for chips in CHIPS)
GROUP = 8
ROWS = (208, 208)
OWN = 24
HALF = 2560
CHUNKS = 4
WIDE = HALF // CHUNKS


def step(chip, to):
    return abs(to[0] - chip[0]), (to[1] - chip[1] + 3) % 8 - 3


def kernel(
    q_hbm, k_hbm, v_hbm, pos_hbm, w_hbm, out_ref,
    q_in, w_in, pos_in, early, late, q_t, high, total, acc, tri,
    part, through, passed, beside, across, crossed,
    load_sem, send_sem, recv_sem, row_send, row_recv,
):
    blk, inner = lax.axis_index("blk"), lax.axis_index("inner")
    ylo, z, core = blk // 16, (blk // 2) % 8, blk % 2
    yhi, x = inner // 4, inner % 4
    bufs = (early, late)

    loads = [
        pltpu.make_async_copy(pos_hbm, pos_in, load_sem.at[6]),
        pltpu.make_async_copy(k_hbm.at[pl.ds(0, CH)], early.at[0, pl.ds(0, CH)], load_sem.at[0]),
        pltpu.make_async_copy(v_hbm.at[pl.ds(0, CH)], early.at[0, pl.ds(CH, CH)], load_sem.at[1]),
        pltpu.make_async_copy(k_hbm.at[pl.ds(CH, CH)], late.at[0, pl.ds(0, CH)], load_sem.at[2]),
        pltpu.make_async_copy(v_hbm.at[pl.ds(CH, CH)], late.at[0, pl.ds(CH, CH)], load_sem.at[3]),
        pltpu.make_async_copy(q_hbm, q_in, load_sem.at[4]),
        pltpu.make_async_copy(w_hbm, w_in, load_sem.at[5]),
    ]
    for load in loads:
        load.start()

    def at(dy, dz, dc=0):
        y = ylo + dy - 2 * dy * ylo
        c = core + dc - 2 * dc * core
        return (y * 16 + lax.rem(z + dz * (1 - 2 * core) + 8, 8) * 2 + c, inner)

    def along(d):
        return (blk, yhi * 4 + lax.rem(x + d + 4, 4))

    opposite = (blk, lax.rem(inner + 4, 8))
    barrier = pltpu.get_barrier_semaphore()
    steps = {step(a, b)[1] for tree in TREES for a, ends in tree.items() for b in ends}
    steps = sorted({d % 8 for d in steps if d} | {-d % 8 for d in steps if d})
    greeted = [at(0, d) for d in steps] + [at(1, 0), at(0, 0, 1)]
    greeted += [along(1), along(-1), opposite]
    for device in greeted:
        pl.semaphore_signal(barrier, inc=1, device_id=device, device_id_type=MESH)

    sends = []

    def send(phase, src, dst, device):
        count = sum(1 for p, _ in sends if p == phase)
        copy = pltpu.make_async_remote_copy(
            src_ref=bufs[phase].at[src],
            dst_ref=bufs[phase].at[dst],
            send_sem=send_sem.at[phase, count],
            recv_sem=recv_sem.at[phase, dst],
            device_id=device,
            device_id_type=MESH,
        )
        copy.start()
        sends.append((phase, copy))

    def arrived(phase, slot):
        ref = bufs[phase].at[slot]
        pltpu.make_async_copy(ref, ref, recv_sem.at[phase, slot]).wait()

    def pass_on(phase, *chips):
        for chip in chips:
            slot = SLOT[phase][chip]
            if chip != (0, 0):
                arrived(phase, slot)
            for to in TREES[phase].get(chip, ()):
                send(phase, slot, SLOT[phase][to], at(*step(chip, to)))
            send(phase, slot, slot + 1, at(0, 0, 1))

    taken = set()

    def from_sibling_once(phase, group):
        if (phase, group) in taken:
            return
        taken.add((phase, group))
        for j in range(4 * group, 4 * group + 4):
            arrived(phase, 2 * j + 1)

    def attend(phase, which, group, first=False):
        buf = bufs[which]
        base = group * GROUP
        keys = buf[pl.ds(base, GROUP), pl.ds(0, CH), :].reshape(GROUP * CH, HEAD)
        values = buf[pl.ds(base, GROUP), pl.ds(CH, CH), :].reshape(GROUP * CH, HEAD)
        scores = jnp.dot(keys, q_t[phase], preferred_element_type=jnp.float32)
        if phase == which:
            tags = buf[pl.ds(base, GROUP), pl.ds(2 * CH, 16), :].astype(jnp.float32)[:, :1, :]
            seen = tags < tag if phase == 0 else tags > tag
            bias = jnp.where(seen, 0.0, LOW)
            bias = jnp.concatenate([bias] * (LANES // HEAD), axis=2)
            scores = scores.reshape(GROUP, CH, LANES)
            if first:
                scores = jnp.concatenate([scores[:1] + tri[...][None], scores[1:] + bias[1:]], axis=0)
            else:
                scores = scores + bias
            scores = scores.reshape(GROUP * CH, LANES)
        old = high[phase]
        new = jnp.maximum(old, jnp.max(scores, axis=0, keepdims=True) * SCALE)
        weights = jnp.exp2(scores * SCALE - new)
        keep = jnp.exp2(old - new)
        high[phase] = new
        total[phase] = total[phase] * keep + jnp.sum(weights, axis=0, keepdims=True)
        mixed = lax.dot_general(
            values, weights.astype(jnp.bfloat16), (((0,), (0,)), ((), ())),
            preferred_element_type=jnp.float32,
        )
        acc[phase] = acc[phase] * keep + mixed

    row_sends = []

    def row_send_to(kind, phase, j, src, dst, device):
        copy = pltpu.make_async_remote_copy(
            src_ref=src, dst_ref=dst.at[phase, j],
            send_sem=row_send.at[kind, phase, j], recv_sem=row_recv.at[kind, phase, j],
            device_id=device, device_id_type=MESH,
        )
        return copy

    def row_wait(kind, phase, j, dst):
        ref = dst.at[phase, j]
        pltpu.make_async_copy(ref, ref, row_recv.at[kind, phase, j]).wait()

    def way(j):
        return 1 if j % 2 == 0 else -1

    def project(phase):
        if phase == 0:
            loads[6].wait()
        rows = jnp.transpose(acc[phase] * (1.0 / total[phase])).astype(jnp.bfloat16)
        rows = jnp.concatenate([rows[h * CH : (h + 1) * CH] for h in range(PER_KEY)], axis=1)
        for piece in range(CHUNKS // 2):
            left, right = [
                jnp.dot(
                    rows, w_in[:, side * HALF + piece * 2 * WIDE : side * HALF + (piece + 1) * 2 * WIDE],
                    preferred_element_type=jnp.float32,
                )
                for side in range(2)
            ]
            for j in (2 * piece, 2 * piece + 1):
                cols = slice((j % 2) * WIDE, (j % 2 + 1) * WIDE)
                for d in range(4):
                    cut = slice(OWN * d, OWN * (d + 1))
                    both = jnp.concatenate([left[cut, cols], right[cut, cols]], axis=0)
                    part[phase, j, d] = both.astype(jnp.bfloat16)
            for j in (2 * piece, 2 * piece + 1):
                s = way(j)
                copy = row_send_to(0, phase, j, part.at[phase, j, lax.rem(x + 2, 4)], through, along(s))
                copy.start()
                row_sends.append(copy)
            for j in (2 * piece, 2 * piece + 1):
                s = way(j)
                copy = row_send_to(1, phase, j, part.at[phase, j, lax.rem(x + 4 - s, 4)], beside, along(-s))
                copy.start()
                row_sends.append(copy)

    def go_through(phase, *chunks):
        for j in chunks:
            s = way(j)
            row_wait(0, phase, j, through)
            mine = part[phase, j, lax.rem(x + 4 + s, 4)].astype(jnp.float32)
            through[phase, j] = (mine + through[phase, j].astype(jnp.float32)).astype(jnp.bfloat16)
            copy = row_send_to(2, phase, j, through.at[phase, j], passed, along(s))
            copy.start()
            row_sends.append(copy)

    def ring_sum(phase, j):
        row_wait(1, phase, j, beside)
        row_wait(2, phase, j, passed)
        summed = part[phase, j, x].astype(jnp.float32) + beside[phase, j].astype(jnp.float32)
        return summed + passed[phase, j].astype(jnp.float32)

    def cross_copy(phase, j):
        return row_send_to(3, phase, j, across.at[phase, j], crossed, opposite)

    def cross(phase, *chunks):
        @pl.when(yhi != phase)
        def _():
            for j in chunks:
                across[phase, j] = ring_sum(phase, j).astype(jnp.bfloat16)
                cross_copy(phase, j).start()

    def finish(phase):
        @pl.when(yhi == phase)
        def _():
            for j in range(CHUNKS):
                summed = ring_sum(phase, j)
                row_wait(3, phase, j, crossed)
                summed = (summed + crossed[phase, j].astype(jnp.float32)).astype(out_ref.dtype)
                out_ref[:, j * WIDE : (j + 1) * WIDE] = summed[:OWN]
                out_ref[:, HALF + j * WIDE : HALF + (j + 1) * WIDE] = summed[OWN:]

        @pl.when(yhi != phase)
        def _():
            for j in range(CHUNKS):
                cross_copy(phase, j).wait_send()

    lane = lax.broadcasted_iota(jnp.int32, (CH, LANES), 1)
    start = sum(jnp.where(lane >= CH * h, CH, 0) for h in range(1, PER_KEY + 1))
    row = lax.broadcasted_iota(jnp.int32, (CH, LANES), 0)
    tri[...] = jnp.where(row <= lane - start, 0.0, LOW)
    high[...] = jnp.full(high.shape, LOW, jnp.float32)
    total[...] = jnp.zeros(total.shape, jnp.float32)
    acc[...] = jnp.zeros(acc.shape, jnp.float32)

    pl.semaphore_wait(barrier, len(greeted))
    loads[0].wait()
    tag = pos_in[0].astype(jnp.float32)
    for buf in bufs:
        buf[0, pl.ds(2 * CH, 16), :] = jnp.full((16, HEAD), tag, jnp.float32).astype(jnp.bfloat16)
    loads[1].wait()
    loads[2].wait()
    pass_on(0, (0, 0))
    loads[3].wait()
    loads[4].wait()
    pass_on(1, (0, 0))
    loads[5].wait()
    for phase in range(2):
        heads = [q_in[pl.ds(CH * phase, CH), pl.ds(HEAD * h, HEAD)] for h in range(PER_KEY)]
        pad = jnp.zeros((LANES - PER_KEY * CH, HEAD), jnp.bfloat16)
        q_t[phase] = jnp.transpose(jnp.concatenate(heads + [pad], axis=0))

    for what, *which in PLAN:
        if what == "take":
            pass_on(*which)
        elif what == "attend":
            phase, side, group = which
            from_sibling_once(side, group)
            attend(phase, side, group, first=phase == side and group == 0)
        elif what == "project":
            project(*which)
        elif what == "cross":
            cross(*which)
        elif what == "through":
            go_through(*which)
    go_through(1, 0, 1)
    go_through(1, 2, 3)
    cross(1, *range(CHUNKS))
    finish(0)
    finish(1)
    for _, copy in sends:
        copy.wait_send()
    for copy in row_sends:
        copy.wait_send()


def shards(queries, keys, values, positions, out_weight):
    any_space = pl.BlockSpec(memory_space=pl.ANY)
    return pl.pallas_call(
        kernel,
        out_shape=jax.ShapeDtypeStruct((OWN, 2 * HALF), jnp.bfloat16),
        in_specs=[any_space] * 5,
        out_specs=pl.BlockSpec(memory_space=pltpu.VMEM),
        scratch_shapes=[
            pltpu.VMEM((2 * CH, PER_KEY * HEAD), jnp.bfloat16),
            pltpu.VMEM((PER_KEY * HEAD, 2 * HALF), jnp.bfloat16),
            pltpu.SMEM((2 * CH,), jnp.int32),
            pltpu.VMEM((32, ROWS[0], HEAD), jnp.bfloat16),
            pltpu.VMEM((32, ROWS[1], HEAD), jnp.bfloat16),
            pltpu.VMEM((2, HEAD, LANES), jnp.bfloat16),
            pltpu.VMEM((2, 1, LANES), jnp.float32),
            pltpu.VMEM((2, 1, LANES), jnp.float32),
            pltpu.VMEM((2, HEAD, LANES), jnp.float32),
            pltpu.VMEM((CH, LANES), jnp.float32),
            pltpu.VMEM((2, CHUNKS, 4, 2 * OWN, WIDE), jnp.bfloat16),
            *[pltpu.VMEM((2, CHUNKS, 2 * OWN, WIDE), jnp.bfloat16) for _ in range(5)],
            pltpu.SemaphoreType.DMA((7,)),
            pltpu.SemaphoreType.DMA((2, 32)),
            pltpu.SemaphoreType.DMA((2, 32)),
            pltpu.SemaphoreType.DMA((4, 2, CHUNKS)),
            pltpu.SemaphoreType.DMA((4, 2, CHUNKS)),
        ],
        compiler_params=pltpu.CompilerParams(
            collective_id=0, has_side_effects=True, vmem_limit_bytes=62 << 20
        ),
        cost_estimate=pl.CostEstimate(
            flops=4_000_000_000, bytes_accessed=10_000_000, transcendentals=5_000_000
        ),
    )(queries, keys, values, positions, out_weight)


def solution(mesh):
    placed = (P("blk", "inner"), P("blk", "inner"), P("blk", "inner"), P("blk"), P("inner", None))
    return jax.shard_map(
        shards, mesh=mesh, in_specs=placed, out_specs=P(("blk", "inner"), None), check_vma=False
    )
```

```python
import math

import jax
import jax.numpy as jnp
from jax import lax
from jax.experimental import pallas as pl
from jax.experimental.pallas import tpu as pltpu
from jax.sharding import PartitionSpec as P

MESH = pl.DeviceIdType.MESH
HEAD = 128
PER_KEY = 5
CH = 96
LANES = 512
SCALE = math.log2(math.e) / math.sqrt(HEAD)
LOW = -1e30

CHIPS = (
    [(0, 0), (0, -1), (1, 0), (0, 2), (0, -2), (1, -1), (1, 1), (0, 3), (1, 2), (1, -3), (1, -2), (0, -3), (0, 1), (0, 4), (1, 4), (1, 3)],
    [(0, 0), (0, -1), (1, 0), (0, 2), (1, -1), (0, 3), (1, -2), (0, 4), (1, 3), (0, 1), (0, -2), (1, -3), (0, -3), (1, 4), (1, 1), (1, 2)],
)
TREES = (
    {
        (0, 0): [(0, -1), (0, 2), (1, 0)],
        (0, -1): [(0, -2), (1, -1)],
        (1, 0): [(1, 1), (1, -3)],
        (0, 2): [(0, 3), (1, 2)],
        (0, -2): [(0, -3), (1, -2)],
        (1, 1): [(0, 1)],
        (0, 3): [(0, 4), (1, 3)],
        (1, -3): [(1, 4)],
    },
    {
        (0, 0): [(0, -1), (0, 2), (1, 0)],
        (0, -1): [(1, -1)],
        (0, 2): [(0, 3)],
        (1, -1): [(1, -2)],
        (0, 3): [(0, 4), (1, 3), (0, 1)],
        (1, -2): [(0, -2), (1, 1), (1, -3)],
        (0, 4): [(0, -3), (1, 4)],
        (1, 3): [(1, 2)],
    },
)
PLAN = [
    ("take", 0, (0, -1), (1, 0)),
    ("take", 1, (0, -1), (1, 0)),
    ("take", 0, (0, 2)),
    ("take", 1, (0, 2)),
    ("take", 0, (0, -2), (1, -1), (1, 1)),
    ("attend", 0, 0, 0),
    ("take", 1, (1, -1)),
    ("attend", 1, 1, 0),
    ("take", 0, (0, 3), (1, 2), (1, -3)),
    ("attend", 1, 0, 0),
    ("take", 1, (0, 3)),
    ("take", 0, (1, -2), (0, -3)),
    ("attend", 0, 0, 1),
    ("take", 1, (1, -2)),
    ("take", 0, (0, 1), (0, 4)),
    ("attend", 0, 0, 2),
    ("take", 0, (1, 4), (1, 3)),
    ("take", 1, (0, 4)),
    ("attend", 1, 0, 1),
    ("take", 1, (1, 3), (0, 1)),
    ("attend", 0, 0, 3),
    ("take", 1, (0, -2), (1, -3)),
    ("project", 0),
    ("take", 1, (0, -3), (1, 4), (1, 1), (1, 2)),
    ("attend", 1, 1, 1),
    ("attend", 1, 1, 2),
    ("through", 0, 0, 1, 2, 3),
    ("attend", 1, 1, 3),
    ("attend", 1, 0, 2),
    ("attend", 1, 0, 3),
    ("cross", 0, 0, 1, 2, 3),
    ("project", 1),
]
SLOT = tuple({chip: 2 * j for j, chip in enumerate(chips)} for chips in CHIPS)
GROUP = 8
ROWS = (208, 208)
OWN = 24
HALF = 2560
CHUNKS = 4
WIDE = HALF // CHUNKS


def step(chip, to):
    return abs(to[0] - chip[0]), (to[1] - chip[1] + 3) % 8 - 3


def kernel(
    q_hbm, k_hbm, v_hbm, pos_hbm, w_hbm, out_ref,
    q_in, w_in, pos_in, early, late, q_t, high, total, acc, tri,
    part, through, passed, beside, across, crossed,
    load_sem, send_sem, recv_sem, row_send, row_recv,
):
    blk, inner = lax.axis_index("blk"), lax.axis_index("inner")
    ylo, z, core = blk // 16, (blk // 2) % 8, blk % 2
    yhi, x = inner // 4, inner % 4
    bufs = (early, late)

    loads = [
        pltpu.make_async_copy(pos_hbm, pos_in, load_sem.at[6]),
        pltpu.make_async_copy(k_hbm.at[pl.ds(0, CH)], early.at[0, pl.ds(0, CH)], load_sem.at[0]),
        pltpu.make_async_copy(v_hbm.at[pl.ds(0, CH)], early.at[0, pl.ds(CH, CH)], load_sem.at[1]),
        pltpu.make_async_copy(k_hbm.at[pl.ds(CH, CH)], late.at[0, pl.ds(0, CH)], load_sem.at[2]),
        pltpu.make_async_copy(v_hbm.at[pl.ds(CH, CH)], late.at[0, pl.ds(CH, CH)], load_sem.at[3]),
        pltpu.make_async_copy(q_hbm, q_in, load_sem.at[4]),
        pltpu.make_async_copy(w_hbm, w_in, load_sem.at[5]),
    ]
    for load in loads:
        load.start()

    def at(dy, dz, dc=0):
        y = ylo + dy - 2 * dy * ylo
        c = core + dc - 2 * dc * core
        return (y * 16 + lax.rem(z + dz * (1 - 2 * core) + 8, 8) * 2 + c, inner)

    def along(d):
        return (blk, yhi * 4 + lax.rem(x + d + 4, 4))

    opposite = (blk, lax.rem(inner + 4, 8))
    barrier = pltpu.get_barrier_semaphore()
    steps = {step(a, b)[1] for tree in TREES for a, ends in tree.items() for b in ends}
    steps = sorted({d % 8 for d in steps if d} | {-d % 8 for d in steps if d})
    greeted = [at(0, d) for d in steps] + [at(1, 0), at(0, 0, 1)]
    greeted += [along(1), along(-1), opposite]
    for device in greeted:
        pl.semaphore_signal(barrier, inc=1, device_id=device, device_id_type=MESH)

    sends = []

    def send(phase, src, dst, device):
        count = sum(1 for p, _ in sends if p == phase)
        copy = pltpu.make_async_remote_copy(
            src_ref=bufs[phase].at[src],
            dst_ref=bufs[phase].at[dst],
            send_sem=send_sem.at[phase, count],
            recv_sem=recv_sem.at[phase, dst],
            device_id=device,
            device_id_type=MESH,
        )
        copy.start()
        sends.append((phase, copy))

    def arrived(phase, slot):
        ref = bufs[phase].at[slot]
        pltpu.make_async_copy(ref, ref, recv_sem.at[phase, slot]).wait()

    def pass_on(phase, *chips):
        for chip in chips:
            slot = SLOT[phase][chip]
            if chip != (0, 0):
                arrived(phase, slot)
            for to in TREES[phase].get(chip, ()):
                send(phase, slot, SLOT[phase][to], at(*step(chip, to)))
            send(phase, slot, slot + 1, at(0, 0, 1))

    taken = set()

    def from_sibling_once(phase, group):
        if (phase, group) in taken:
            return
        taken.add((phase, group))
        for j in range(4 * group, 4 * group + 4):
            arrived(phase, 2 * j + 1)

    def attend(phase, which, group, first=False):
        buf = bufs[which]
        base = group * GROUP
        keys = buf[pl.ds(base, GROUP), pl.ds(0, CH), :].reshape(GROUP * CH, HEAD)
        values = buf[pl.ds(base, GROUP), pl.ds(CH, CH), :].reshape(GROUP * CH, HEAD)
        scores = jnp.dot(keys, q_t[phase], preferred_element_type=jnp.float32)
        if phase == which:
            tags = buf[pl.ds(base, GROUP), pl.ds(2 * CH, 16), :].astype(jnp.float32)[:, :1, :]
            seen = tags < tag if phase == 0 else tags > tag
            bias = jnp.where(seen, 0.0, LOW)
            bias = jnp.concatenate([bias] * (LANES // HEAD), axis=2)
            scores = scores.reshape(GROUP, CH, LANES)
            if first:
                scores = jnp.concatenate([scores[:1] + tri[...][None], scores[1:] + bias[1:]], axis=0)
            else:
                scores = scores + bias
            scores = scores.reshape(GROUP * CH, LANES)
        old = high[phase]
        new = jnp.maximum(old, jnp.max(scores, axis=0, keepdims=True) * SCALE)
        weights = jnp.exp2(scores * SCALE - new)
        keep = jnp.exp2(old - new)
        high[phase] = new
        total[phase] = total[phase] * keep + jnp.sum(weights, axis=0, keepdims=True)
        mixed = lax.dot_general(
            values, weights.astype(jnp.bfloat16), (((0,), (0,)), ((), ())),
            preferred_element_type=jnp.float32,
        )
        acc[phase] = acc[phase] * keep + mixed

    row_sends = []

    def row_send_to(kind, phase, j, src, dst, device):
        copy = pltpu.make_async_remote_copy(
            src_ref=src, dst_ref=dst.at[phase, j],
            send_sem=row_send.at[kind, phase, j], recv_sem=row_recv.at[kind, phase, j],
            device_id=device, device_id_type=MESH,
        )
        return copy

    def row_wait(kind, phase, j, dst):
        ref = dst.at[phase, j]
        pltpu.make_async_copy(ref, ref, row_recv.at[kind, phase, j]).wait()

    def way(j):
        return 1 if j % 2 == 0 else -1

    def project(phase):
        if phase == 0:
            loads[6].wait()
        rows = jnp.transpose(acc[phase] * (1.0 / total[phase])).astype(jnp.bfloat16)
        rows = jnp.concatenate([rows[h * CH : (h + 1) * CH] for h in range(PER_KEY)], axis=1)
        for piece in range(CHUNKS // 2):
            left, right = [
                jnp.dot(
                    rows, w_in[:, side * HALF + piece * 2 * WIDE : side * HALF + (piece + 1) * 2 * WIDE],
                    preferred_element_type=jnp.float32,
                )
                for side in range(2)
            ]
            for j in (2 * piece, 2 * piece + 1):
                cols = slice((j % 2) * WIDE, (j % 2 + 1) * WIDE)
                for d in range(4):
                    cut = slice(OWN * d, OWN * (d + 1))
                    both = jnp.concatenate([left[cut, cols], right[cut, cols]], axis=0)
                    part[phase, j, d] = both.astype(jnp.bfloat16)
            for j in (2 * piece, 2 * piece + 1):
                s = way(j)
                copy = row_send_to(0, phase, j, part.at[phase, j, lax.rem(x + 2, 4)], through, along(s))
                copy.start()
                row_sends.append(copy)
            for j in (2 * piece, 2 * piece + 1):
                s = way(j)
                copy = row_send_to(1, phase, j, part.at[phase, j, lax.rem(x + 4 - s, 4)], beside, along(-s))
                copy.start()
                row_sends.append(copy)

    def go_through(phase, *chunks):
        for j in chunks:
            s = way(j)
            row_wait(0, phase, j, through)
            mine = part[phase, j, lax.rem(x + 4 + s, 4)].astype(jnp.float32)
            through[phase, j] = (mine + through[phase, j].astype(jnp.float32)).astype(jnp.bfloat16)
            copy = row_send_to(2, phase, j, through.at[phase, j], passed, along(s))
            copy.start()
            row_sends.append(copy)

    def ring_sum(phase, j):
        row_wait(1, phase, j, beside)
        row_wait(2, phase, j, passed)
        summed = part[phase, j, x].astype(jnp.float32) + beside[phase, j].astype(jnp.float32)
        return summed + passed[phase, j].astype(jnp.float32)

    def cross_copy(phase, j):
        return row_send_to(3, phase, j, across.at[phase, j], crossed, opposite)

    def cross(phase, *chunks):
        @pl.when(yhi != phase)
        def _():
            for j in chunks:
                across[phase, j] = ring_sum(phase, j).astype(jnp.bfloat16)
                cross_copy(phase, j).start()

    def finish(phase):
        @pl.when(yhi == phase)
        def _():
            for j in range(CHUNKS):
                summed = ring_sum(phase, j)
                row_wait(3, phase, j, crossed)
                summed = (summed + crossed[phase, j].astype(jnp.float32)).astype(out_ref.dtype)
                out_ref[:, j * WIDE : (j + 1) * WIDE] = summed[:OWN]
                out_ref[:, HALF + j * WIDE : HALF + (j + 1) * WIDE] = summed[OWN:]

        @pl.when(yhi != phase)
        def _():
            for j in range(CHUNKS):
                cross_copy(phase, j).wait_send()

    lane = lax.broadcasted_iota(jnp.int32, (CH, LANES), 1)
    start = sum(jnp.where(lane >= CH * h, CH, 0) for h in range(1, PER_KEY + 1))
    row = lax.broadcasted_iota(jnp.int32, (CH, LANES), 0)
    tri[...] = jnp.where(row <= lane - start, 0.0, LOW)
    high[...] = jnp.full(high.shape, LOW, jnp.float32)
    total[...] = jnp.zeros(total.shape, jnp.float32)
    acc[...] = jnp.zeros(acc.shape, jnp.float32)

    pl.semaphore_wait(barrier, len(greeted))
    loads[0].wait()
    tag = pos_in[0].astype(jnp.float32)
    for buf in bufs:
        buf[0, pl.ds(2 * CH, 16), :] = jnp.full((16, HEAD), tag, jnp.float32).astype(jnp.bfloat16)
    loads[1].wait()
    loads[2].wait()
    pass_on(0, (0, 0))
    loads[3].wait()
    loads[4].wait()
    pass_on(1, (0, 0))
    loads[5].wait()
    for phase in range(2):
        heads = [q_in[pl.ds(CH * phase, CH), pl.ds(HEAD * h, HEAD)] for h in range(PER_KEY)]
        pad = jnp.zeros((LANES - PER_KEY * CH, HEAD), jnp.bfloat16)
        q_t[phase] = jnp.transpose(jnp.concatenate(heads + [pad], axis=0))

    for what, *which in PLAN:
        if what == "take":
            pass_on(*which)
        elif what == "attend":
            phase, side, group = which
            from_sibling_once(side, group)
            attend(phase, side, group, first=phase == side and group == 0)
        elif what == "project":
            project(*which)
        elif what == "cross":
            cross(*which)
        elif what == "through":
            go_through(*which)
    go_through(1, 0, 1)
    go_through(1, 2, 3)
    cross(1, *range(CHUNKS))
    finish(0)
    finish(1)
    for _, copy in sends:
        copy.wait_send()
    for copy in row_sends:
        copy.wait_send()


def shards(queries, keys, values, positions, out_weight):
    any_space = pl.BlockSpec(memory_space=pl.ANY)
    return pl.pallas_call(
        kernel,
        out_shape=jax.ShapeDtypeStruct((OWN, 2 * HALF), jnp.bfloat16),
        in_specs=[any_space] * 5,
        out_specs=pl.BlockSpec(memory_space=pltpu.VMEM),
        scratch_shapes=[
            pltpu.VMEM((2 * CH, PER_KEY * HEAD), jnp.bfloat16),
            pltpu.VMEM((PER_KEY * HEAD, 2 * HALF), jnp.bfloat16),
            pltpu.SMEM((2 * CH,), jnp.int32),
            pltpu.VMEM((32, ROWS[0], HEAD), jnp.bfloat16),
            pltpu.VMEM((32, ROWS[1], HEAD), jnp.bfloat16),
            pltpu.VMEM((2, HEAD, LANES), jnp.bfloat16),
            pltpu.VMEM((2, 1, LANES), jnp.float32),
            pltpu.VMEM((2, 1, LANES), jnp.float32),
            pltpu.VMEM((2, HEAD, LANES), jnp.float32),
            pltpu.VMEM((CH, LANES), jnp.float32),
            pltpu.VMEM((2, CHUNKS, 4, 2 * OWN, WIDE), jnp.bfloat16),
            *[pltpu.VMEM((2, CHUNKS, 2 * OWN, WIDE), jnp.bfloat16) for _ in range(5)],
            pltpu.SemaphoreType.DMA((7,)),
            pltpu.SemaphoreType.DMA((2, 32)),
            pltpu.SemaphoreType.DMA((2, 32)),
            pltpu.SemaphoreType.DMA((4, 2, CHUNKS)),
            pltpu.SemaphoreType.DMA((4, 2, CHUNKS)),
        ],
        compiler_params=pltpu.CompilerParams(
            collective_id=0, has_side_effects=True, vmem_limit_bytes=62 << 20
        ),
        cost_estimate=pl.CostEstimate(
            flops=4_000_000_000, bytes_accessed=10_000_000, transcendentals=5_000_000
        ),
    )(queries, keys, values, positions, out_weight)


def solution(mesh):
    placed = (P("blk", "inner"), P("blk", "inner"), P("blk", "inner"), P("blk"), P("inner", None))
    return jax.shard_map(
        shards, mesh=mesh, in_specs=placed, out_specs=P(("blk", "inner"), None), check_vma=False
    )
```
